128 devices in a mesh: doc: 8 (over x, y_hi), param: 16 (over z, y_lo, core).
Axes of the slice: x: 4, y: 4 (y_hi: 2, y_lo: 2; y = y_hi * 2 + y_lo), z: 4, core: 2. Of those that a mesh axis runs over, the one named last changes fastest.
Arguments:
- activations: bfloat16 [512, 128, 13824], P('doc', None, 'param'), may hold values from -6 to 6
- out_grads: bfloat16 [512, 128, 5120], P('doc', None, 'param'), may hold values from -6 to 6
- proj_in: bfloat16 [64, 13824], P(None, 'param'), may hold values from -0.0546875 to 0.0546875
- proj_out: bfloat16 [64, 5120], P(None, 'param'), may hold values from -0.078125 to 0.078125
- lengths: int32 [512], P('doc'), may hold values from 1 to 128, as said below
- loss_mask: int32 [512, 128], P('doc'), may hold values 0 or 1
- queries: float32 [1024, 4096], P(('doc', 'param')), may hold values from -6 to 6
- left_pre: float32 [64, 64], replicated, may hold values from -0.75 to 0.75
- right_pre: float32 [64, 64], replicated, may hold values from -0.75 to 0.75
Outputs:
- scores: float32 [512, 1024], P(('doc', 'param'))
The draws below stay inside these ranges and needn't reach their ends.
Inputs may be any that keep to these rules, and one draw needn't show every extreme that they name: `lengths`: some document has 128 tokens and some has 1.
All inputs are finite; a program needn't handle non-finite values. No bound on the sum of `loss_mask` on one device may be relied on, other than what follows from the above.
Results may differ from the reference program's by a relative error of at most 0.0003.
Values sent between devices are 32-bit elements; how exact they have to be, the bound alone decides.
A program may use at most 128 MiB of HBM per device.

```python
import jax
import jax.numpy as jnp
from jax import lax

D = 5120
FF = 13824
R = 64
SEQ = 128
DOCS = 512
QUERIES = 1024


def draw_lengths(key, part):
    key = jax.random.fold_in(key, 11)
    values = jax.random.randint(key, (DOCS,), 1, SEQ + 1)
    place = jnp.arange(DOCS, dtype=jnp.int32)
    values = jnp.where(place == 0, SEQ, values)
    values = jnp.where(place == 1, 1, values)
    return values.astype(jnp.int32)


def plant(values, stream_key, least, high):
    shape = values.shape
    spot = [jax.random.randint(jax.random.fold_in(stream_key, axis), (), 0, shape[axis]) for axis in range(len(shape))]
    values = values.at[tuple(spot)].set(least)
    longest = shape.index(max(shape))
    spot[longest] = (spot[longest] + 1) % shape[longest]
    return values.at[tuple(spot)].set(high)


def levels(stream_key, dims, pieces, smallest, top_value):
    loudness = 1.0
    for dim, parts in pieces:
        heights = jax.random.uniform(jax.random.fold_in(jax.random.fold_in(stream_key, 6), dim), (parts,), jnp.float32, smallest / len(pieces), top_value / len(pieces))
        loudness = loudness * jnp.repeat(jnp.exp(heights), dims[dim] // parts).reshape((-1,) + (1,) * (len(dims) - 1 - dim))
    return loudness


def gaussian(rng, extent, deviation, limit, cuts=(), kind=jnp.bfloat16):
    level = levels(rng, extent, cuts, -0.22, 0.18) if cuts else 1.0
    array = jax.random.normal(rng, extent, jnp.float32) * deviation * level
    return jnp.minimum(jnp.maximum(array, -limit), limit).astype(kind)


def setup_inputs(seed: int = 0) -> dict:
    splits = jax.random.split(jax.random.key(seed), 10)
    activations = gaussian(splits[0], (DOCS, SEQ, FF), 1.0, 6.0, ((0, 8), (2, 16)))
    out_grads = gaussian(splits[1], (DOCS, SEQ, D), 1.0, 6.0, ((0, 8), (2, 16)))
    proj_in = gaussian(splits[2], (R, FF), FF ** -0.5, 0.0546875, ((1, 16),))
    proj_out = gaussian(splits[3], (R, D), D ** -0.5, 0.078125, ((1, 16),))
    lengths = draw_lengths(jax.random.fold_in(splits[9], 71), 0)
    loss_mask = plant((jax.random.randint(splits[5], (DOCS, SEQ), 0, 4) < 3).astype(jnp.int32), jax.random.fold_in(splits[5], 1), 0, 1)
    queries = gaussian(splits[6], (QUERIES, R * R), 1.0, 6.0, ((0, 128),), jnp.float32)
    left_pre = gaussian(splits[7], (R, R), R ** -0.5, 0.75, (), jnp.float32)
    right_pre = gaussian(splits[8], (R, R), R ** -0.5, 0.75, (), jnp.float32)
    return {"activations": activations, "out_grads": out_grads, "proj_in": proj_in, "proj_out": proj_out, "lengths": lengths, "loss_mask": loss_mask, "queries": queries, "left_pre": left_pre, "right_pre": right_pre}


def project_block(pair, proj_in, proj_out):
    acts, grads = pair
    in_proj = jnp.einsum('dsh,rh->dsr', acts.astype(jnp.float32), proj_in.astype(jnp.float32))
    out_proj = jnp.einsum('dsh,rh->dsr', grads.astype(jnp.float32), proj_out.astype(jnp.float32))
    return (in_proj, out_proj)

def reference(activations, out_grads, proj_in, proj_out, lengths, loss_mask, queries, left_pre, right_pre):
    group = 16
    acts = activations.reshape(DOCS // group, group, SEQ, FF)
    grads = out_grads.reshape(DOCS // group, group, SEQ, D)
    in_proj, out_proj = lax.map(lambda pair: project_block(pair, proj_in, proj_out), (acts, grads))
    in_proj = in_proj.reshape(DOCS, SEQ, R)
    out_proj = out_proj.reshape(DOCS, SEQ, R)
    slots = jnp.arange(SEQ, dtype=jnp.int32)[None, :]
    weight = loss_mask.astype(jnp.float32) * (slots < lengths[:, None]).astype(jnp.float32)
    doc_grad = jnp.einsum('dso,dsi->doi', out_proj * weight[:, :, None], in_proj, precision=lax.Precision.HIGHEST)
    doc_grad = doc_grad.reshape(DOCS, R * R)
    square = queries.reshape(QUERIES, R, R)
    left = jnp.einsum('ab,qbc->qac', left_pre, square, precision=lax.Precision.HIGHEST)
    precond = jnp.einsum('qac,cd->qad', left, right_pre, precision=lax.Precision.HIGHEST).reshape(QUERIES, R * R)
    scale = 1.0 / (R * jnp.sqrt(jnp.float32(SEQ)))
    return jnp.dot(doc_grad, precond.T, precision=lax.Precision.HIGHEST) * scale
```

```python
import functools

import jax
import jax.numpy as jnp
from jax import lax
from jax.experimental import pallas as pl
from jax.experimental.pallas import tpu as pltpu
from jax.sharding import PartitionSpec as P

MESH = pl.DeviceIdType.MESH
F32 = jnp.float32
BF16 = jnp.bfloat16
HIGHEST = lax.Precision.HIGHEST

RANK = 64
SEQ = 128
OWNED = 4
ROWS = OWNED * SEQ
HALF_A = 144
HALF_B = 112
PART_A = 2 * HALF_A
AHEAD = 3
ORDER = ((2, 0), (2, 1), (1, 0), (1, 1), (3, 0), (3, 1), (0, 0), (0, 1))
PLACE = {step: j for j, step in enumerate(ORDER)}
PEERS = tuple(
    (dz, dy, dc) for dz in (2, 1, 3, 0) for dy in (1, 0) for dc in (1, 0) if (dz, dy, dc) != (0, 0, 0)
)
N_SEMS = 8 + 18 + 5 + 15 + 1 + 3 + 15 + 15


def iota(shape, dim):
    return lax.broadcasted_iota(jnp.int32, shape, dim)


def split(x):
    high = x.astype(BF16)
    return high, (x - high.astype(F32)).astype(BF16)


def dot(a, b, contract=(1, 0), precision=None):
    return lax.dot_general(
        a, b, (((contract[0],), (contract[1],)), ((), ())), precision=precision, preferred_element_type=F32
    )


def kernel(
    act, grad, pin, pout, lengths, mask, queries, left, right,
    out,
    act_v, grad_v, pin_v, pout_v, len_s, mask_v, q_v, left_v, right_v, w_in, w_out,
    blocks, twin, f_a, n_a, f_b, n_b, y_a, y_b,
    t_own, t_all, t_high, t_low, g_own, g_all, s_own, s_all,
    load_sem, small_sem, send_sem, recv_sem,
):
    doc, me = lax.axis_index("doc"), lax.axis_index("param")
    x, hi = doc // 2, lax.rem(doc, 2)
    z, lo, core = me // 4, lax.rem(me // 2, 2), lax.rem(me, 2)

    def place(dz, dy, dc):
        py = 1 - lo if dy else lo
        pc = 1 - core if dc else core
        return lax.rem(z + dz, 4) * 4 + py * 2 + pc

    def part(param):
        pz, py, pc = param // 4, lax.rem(param // 2, 2), lax.rem(param, 2)
        return pz * 4 + (py + hi - 2 * py * hi) * 2 + pc

    def loads(j):
        dz, own = ORDER[j]
        found = []
        for r in (1, 0):
            first = place(dz, 1 - own, r) * OWNED
            found.append(pltpu.make_async_copy(act.at[pl.ds(first, OWNED)], act_v.at[j, r], load_sem.at[j, r, 0]))
            found.append(pltpu.make_async_copy(grad.at[pl.ds(first, OWNED)], grad_v.at[j, r], load_sem.at[j, r, 1]))
        return found

    small = [
        pltpu.make_async_copy(src, dst, small_sem.at[i])
        for i, (src, dst) in enumerate(
            (
                (pin, pin_v), (pout, pout_v), (queries, q_v), (left, left_v), (right, right_v),
                (mask, mask_v), (lengths, len_s),
            )
        )
    ]
    small[0].start()
    small[1].start()
    for copy in loads(0):
        copy.start()
    for copy in small[2:]:
        copy.start()
    for j in range(1, AHEAD):
        for copy in loads(j):
            copy.start()

    barrier = pltpu.get_barrier_semaphore()
    greet = [(doc, place(*peer)) for peer in PEERS]
    greet += [(lax.rem(x + dx, 4) * 2 + hi, me) for dx in (1, 2, 3)]
    y_next = (x * 2 + 1 - hi, place(0, 1, 0))
    greet.append(y_next)
    for device in greet:
        pl.semaphore_signal(barrier, inc=1, device_id=device, device_id_type=MESH)

    small[0].wait()
    small[1].wait()
    r_, c_ = iota((RANK, 128), 0), iota((RANK, 128), 1)
    odd = (c_ >= 32).astype(jnp.int32)
    pick_out = jnp.where((c_ < RANK) & (r_ == 2 * (c_ - 32 * odd) + odd), 1.0, 0.0).astype(BF16)
    pick_in = jnp.where(c_ == r_ + RANK, 1.0, 0.0).astype(BF16)
    w_out[...] = dot(pout_v[...], pick_out, (0, 0)).astype(BF16)
    w_in[...] = dot(pin_v[...], pick_in, (0, 0)).astype(BF16)

    counter = [0]
    sent = []

    def send(src, dst, device):
        i = counter[0]
        counter[0] += 1
        copy = pltpu.make_async_remote_copy(
            src_ref=src, dst_ref=dst, send_sem=send_sem.at[i], recv_sem=recv_sem.at[i],
            device_id=device, device_id_type=MESH,
        )
        copy.start()
        sent.append(copy)
        return copy

    up, down = (doc, place(1, 0, 0)), (doc, place(3, 0, 0))
    twin_id, y_id = (doc, place(0, 0, 1)), (doc, place(0, 1, 0))
    core_copy, y_copy, z_copy = {}, {}, {}

    def project(j):
        for copy in loads(j):
            copy.wait()

        def one(i, carry):
            r = 1 - i
            a = act_v[j, r].reshape(ROWS, act_v.shape[-1])
            g = grad_v[j, r].reshape(ROWS, grad_v.shape[-1])
            blocks[j, r] = dot(a, w_in[...]) + dot(g, w_out[...])
            return carry

        lax.fori_loop(0, 2, one, 0)
        core_copy[j] = send(blocks.at[j, 1], twin.at[j], twin_id)

    def ref(t, dz, half):
        if t < 2:
            return blocks.at[PLACE[dz, t], 0, pl.ds(half * HALF_A, HALF_A)]
        return blocks.at[PLACE[dz, 1], 0, pl.ds(PART_A + half * HALF_B, HALF_B)]

    def far(t, half):
        return f_a.at[t, half] if t < 2 else f_b.at[half]

    def near(t, side, half):
        return n_a.at[t, side, half] if t < 2 else n_b.at[side, half]

    def send_far(t):
        z_copy[t, "f0"] = send(ref(t, 2, 0), far(t, 0), up)
        z_copy[t, "f1"] = send(ref(t, 2, 1), far(t, 1), down)

    def send_up_now(t):
        z_copy[t, "u1"] = send(ref(t, 1, 1), near(t, 0, 1), up)

    def send_down_now(t):
        z_copy[t, "d0"] = send(ref(t, 3, 0), near(t, 1, 0), down)

    def send_up_sum(t):
        z_copy[t, "f0"].wait_recv()
        ref(t, 1, 0)[...] += far(t, 0)[...]
        z_copy[t, "u0"] = send(ref(t, 1, 0), near(t, 0, 0), up)

    def send_down_sum(t):
        z_copy[t, "f1"].wait_recv()
        ref(t, 3, 1)[...] += far(t, 1)[...]
        z_copy[t, "d1"] = send(ref(t, 3, 1), near(t, 1, 1), down)

    def finish(t):
        for name in ("u1", "d0", "u0", "d1"):
            z_copy[t, name].wait_recv()
        for half in (0, 1):
            ref(t, 0, half)[...] += near(t, 0, half)[...] + near(t, 1, half)[...]

    def collect(j):
        dz, own = ORDER[j]
        core_copy[j].wait_recv()
        blocks[j, 0] += twin[j]
        if not own:
            y_copy[dz] = send(blocks.at[j, 0, pl.ds(PART_A, ROWS - PART_A)], y_b.at[dz], y_id)
        if dz == 2:
            send_far(own)
        elif dz == 1:
            send_up_now(own)
        elif dz == 3:
            send_down_now(own)

    def y_sum(dz):
        y_copy[dz].wait_recv()
        blocks[PLACE[dz, 1], 0, PART_A:ROWS] += y_b[dz]

    def precondition():
        for copy in small[2:5]:
            copy.wait()
        for m in range(32):
            t_own[m] = q_v[:, m * 128 : (m + 1) * 128]
        wide = jnp.where(lax.rem(iota((128, RANK), 0), RANK) == iota((128, RANK), 1), 1.0, 0.0)
        same = (iota((128, 128), 0) // RANK) == (iota((128, 128), 1) // RANK)
        both = dot(dot(wide, right_v[...], precision=HIGHEST), wide, (1, 1), precision=HIGHEST)
        both = jnp.where(same, both, 0.0)
        u = dot(t_own[...].reshape(256, 128), both, precision=HIGHEST)
        row, col = iota((256, RANK), 0), iota((256, RANK), 1)
        same_q = lax.rem(iota((256, 256), 0), 8) == lax.rem(iota((256, 256), 1), 8)
        take = [jnp.where(col == 2 * (row // 8) + e, 1.0, 0.0) for e in (0, 1)]
        lane = iota((256, 128), 1)
        halves = []
        for e_out in (0, 1):
            rows = dot(take[e_out], left_v[...], precision=HIGHEST)
            pieces = []
            for e_in in (0, 1):
                a = jnp.where(same_q, dot(rows, take[e_in], (1, 1), precision=HIGHEST), 0.0)
                pieces.append(dot(a, u, precision=HIGHEST))
            halves.append(pieces)
        low = halves[0][0] + pltpu.roll(halves[0][1], RANK, 1)
        high = pltpu.roll(halves[1][0], RANK, 1) + halves[1][1]
        t_own[...] = jnp.where(lane < RANK, low, high).reshape(32, 8, 128)

    t_copy = []

    def spread_queries():
        for peer in PEERS:
            param = place(*peer)
            t_copy.append(
                send(t_own.at[pl.ds(2 * part(param), 2)], t_all.at[:, doc, me], (doc, param))
            )
        mine = part(me)
        for m in (0, 1):
            t_all[m, doc, me] = t_own[2 * mine + m]

    def spread_y():
        for copy in t_copy:
            copy.wait_recv()
        return send(t_all.at[:, doc], t_all.at[:, doc], y_next)

    def spread_x(copy):
        copy.wait_recv()
        return [
            send(t_all.at[:, pl.ds(2 * x, 2)], t_all.at[:, pl.ds(2 * x, 2)], (lax.rem(x + dx, 4) * 2 + hi, me))
            for dx in (2, 1, 3)
        ]

    def chunk(j):
        if j + AHEAD < len(ORDER):
            for copy in loads(j + AHEAD):
                copy.start()
        if j == 0:
            pl.semaphore_wait(barrier, len(greet))
        project(j)

    chunk(0)
    chunk(1)
    collect(0)
    chunk(2)
    collect(1)
    precondition()
    spread_queries()
    collect(2)
    chunk(3)
    collect(3)
    chunk(4)
    send_up_sum(0)
    collect(4)
    send_down_sum(0)
    chunk(5)
    send_up_sum(1)
    collect(5)
    send_down_sum(1)
    y_sum(2)
    send_far(2)
    t_y = spread_y()
    chunk(6)
    collect(6)
    chunk(7)
    collect(7)
    y_sum(1)
    send_up_now(2)
    y_sum(3)
    send_down_now(2)
    t_x = spread_x(t_y)
    send_up_sum(2)
    send_down_sum(2)
    finish(0)
    last = send(blocks.at[PLACE[0, 0], 0, pl.ds(0, PART_A)], y_a, y_id)
    finish(1)
    for copy in t_x:
        copy.wait_recv()
    for m in (0, 1):
        high, low = split(t_all[m].reshape(1024, 128))
        t_high[:, m * 128 : (m + 1) * 128] = high
        t_low[:, m * 128 : (m + 1) * 128] = low
    y_sum(0)
    finish(2)
    last.wait_recv()
    home = PLACE[0, 1]
    blocks[home, 0, 0:PART_A] += y_a[...]

    for copy in small[5:]:
        copy.wait()
    lane = iota((SEQ, 128), 1)
    for d in range(OWNED):
        both = blocks[home, 0, d * SEQ : (d + 1) * SEQ]
        row = me * OWNED + d
        weight = jnp.where(iota((1, SEQ), 1) < len_s[row], mask_v[pl.ds(row, 1), :].astype(F32), 0.0)
        high, low = split(both.T[:RANK] * weight)
        lhs = jnp.concatenate([high, low], axis=0)
        in_high = both.astype(BF16).astype(F32)
        rhs = jnp.where(lane >= RANK, in_high, pltpu.roll(both - in_high, RANK, 1)).astype(BF16)
        prod = dot(lhs, rhs)
        prod = prod[:RANK] + prod[RANK:]
        prod = prod + pltpu.roll(prod, RANK, 1)
        whole = jnp.where(lane[:32] < RANK, prod[:32], prod[32:])
        for k in range(16):
            g_own[k, 2 * d : 2 * d + 2] = whole[2 * k : 2 * k + 2]

    g_copy = []
    for peer in PEERS:
        param = place(*peer)
        g_copy.append(send(g_own.at[part(param)], g_all.at[pl.ds(pl.multiple_of(me * 8, 8), 8)], (doc, param)))
    g_all[pl.ds(pl.multiple_of(me * 8, 8), 8), :] = g_own[part(me)]
    for copy in g_copy:
        copy.wait_recv()

    docs = jnp.concatenate([g_all[pl.ds(m, 64, stride=2), :] for m in (0, 1)], axis=1)
    high, low = split(docs)
    scores = dot(jnp.concatenate([high, low], axis=0), t_high[...], (1, 1))
    scores = scores[:64] + scores[64:] + dot(high, t_low[...], (1, 1))
    scores = scores * (1.0 / (RANK * SEQ**0.5))
    for k in range(16):
        s_own[k] = scores[OWNED * k : OWNED * (k + 1)]
    s_copy = []
    for peer in PEERS:
        param = place(*peer)
        s_copy.append(send(s_own.at[param], s_all.at[me], (doc, param)))
    s_all[me] = s_own[me]
    for copy in s_copy:
        copy.wait_recv()
    total = s_all[0]
    for k in range(1, 16):
        total = total + s_all[k]
    out[...] = total
    for copy in sent:
        copy.wait_send()


def body(activations, out_grads, proj_in, proj_out, lengths, loss_mask, queries, left_pre, right_pre):
    wide_in, wide_out = activations.shape[-1], out_grads.shape[-1]
    vmem = pltpu.VMEM
    return pl.pallas_call(
        kernel,
        out_shape=jax.ShapeDtypeStruct((OWNED, 1024), F32),
        in_specs=[pl.BlockSpec(memory_space=pl.ANY)] * 9,
        out_specs=pl.BlockSpec(memory_space=pltpu.VMEM),
        scratch_shapes=[
            vmem((8, 2, OWNED, SEQ, wide_in), BF16),
            vmem((8, 2, OWNED, SEQ, wide_out), BF16),
            vmem(proj_in.shape, BF16),
            vmem(proj_out.shape, BF16),
            pltpu.SMEM(lengths.shape, jnp.int32),
            vmem(loss_mask.shape, jnp.int32),
            vmem(queries.shape, F32),
            vmem(left_pre.shape, F32),
            vmem(right_pre.shape, F32),
            vmem((wide_in, 128), BF16),
            vmem((wide_out, 128), BF16),
            vmem((8, 2, ROWS, 128), F32),
            vmem((8, ROWS, 128), F32),
            vmem((2, 2, HALF_A, 128), F32),
            vmem((2, 2, 2, HALF_A, 128), F32),
            vmem((2, HALF_B, 128), F32),
            vmem((2, 2, HALF_B, 128), F32),
            vmem((PART_A, 128), F32),
            vmem((4, ROWS - PART_A, 128), F32),
            vmem((32, 8, 128), F32),
            vmem((2, 8, 16, 8, 128), F32),
            vmem((1024, 256), BF16),
            vmem((1024, 256), BF16),
            vmem((16, 8, 128), F32),
            vmem((128, 128), F32),
            vmem((16, OWNED, 1024), F32),
            vmem((16, OWNED, 1024), F32),
            pltpu.SemaphoreType.DMA((8, 2, 2)),
            pltpu.SemaphoreType.DMA((7,)),
            pltpu.SemaphoreType.DMA((N_SEMS,)),
            pltpu.SemaphoreType.DMA((N_SEMS,)),
        ],
        compiler_params=pltpu.CompilerParams(
            collective_id=0, has_side_effects=True, vmem_limit_bytes=60 * 1024 * 1024
        ),
        cost_estimate=pl.CostEstimate(flops=1_300_000_000, bytes_accessed=20_000_000, transcendentals=0),
    )(activations, out_grads, proj_in, proj_out, lengths, loss_mask, queries, left_pre, right_pre)


def solution(mesh):
    return jax.shard_map(
        body,
        mesh=mesh,
        in_specs=(
            P("doc", None, "param"),
            P("doc", None, "param"),
            P(None, "param"),
            P(None, "param"),
            P("doc"),
            P("doc", None),
            P(("doc", "param"), None),
            P(),
            P(),
        ),
        out_specs=P(("doc", "param"), None),
        check_vma=False,
    )
```

```python
import functools

import jax
import jax.numpy as jnp
from jax import lax
from jax.experimental import pallas as pl
from jax.experimental.pallas import tpu as pltpu
from jax.sharding import PartitionSpec as P

MESH = pl.DeviceIdType.MESH
F32 = jnp.float32
BF16 = jnp.bfloat16
HIGHEST = lax.Precision.HIGHEST

RANK = 64
SEQ = 128
OWNED = 4
ROWS = OWNED * SEQ
HALF_A = 144
HALF_B = 112
PART_A = 2 * HALF_A
AHEAD = 3
ORDER = ((2, 0), (2, 1), (1, 0), (1, 1), (3, 0), (3, 1), (0, 0), (0, 1))
PLACE = {step: j for j, step in enumerate(ORDER)}
PEERS = tuple(
    (dz, dy, dc) for dz in (2, 1, 3, 0) for dy in (1, 0) for dc in (1, 0) if (dz, dy, dc) != (0, 0, 0)
)
N_SEMS = 8 + 18 + 5 + 15 + 1 + 3 + 15 + 15


def iota(shape, dim):
    return lax.broadcasted_iota(jnp.int32, shape, dim)


def split(x):
    high = x.astype(BF16)
    return high, (x - high.astype(F32)).astype(BF16)


def dot(a, b, contract=(1, 0), precision=None):
    return lax.dot_general(
        a, b, (((contract[0],), (contract[1],)), ((), ())), precision=precision, preferred_element_type=F32
    )


def kernel(
    act, grad, pin, pout, lengths, mask, queries, left, right,
    out,
    act_v, grad_v, pin_v, pout_v, len_s, mask_v, q_v, left_v, right_v, w_out,
    blocks, twin, f_a, n_a, f_b, n_b, y_a, y_b,
    t_own, t_all, t_high, t_low, g_own, g_all, s_own, s_all,
    load_sem, small_sem, send_sem, recv_sem,
):
    doc, me = lax.axis_index("doc"), lax.axis_index("param")
    x, hi = doc // 2, lax.rem(doc, 2)
    z, lo, core = me // 4, lax.rem(me // 2, 2), lax.rem(me, 2)

    def place(dz, dy, dc):
        py = 1 - lo if dy else lo
        pc = 1 - core if dc else core
        return lax.rem(z + dz, 4) * 4 + py * 2 + pc

    def part(param):
        pz, py, pc = param // 4, lax.rem(param // 2, 2), lax.rem(param, 2)
        return pz * 4 + (py + hi - 2 * py * hi) * 2 + pc

    def loads(j):
        dz, own = ORDER[j]
        found = []
        for r in (1, 0):
            first = place(dz, 1 - own, r) * OWNED
            found.append(pltpu.make_async_copy(act.at[pl.ds(first, OWNED)], act_v.at[j, r], load_sem.at[j, r, 0]))
            found.append(pltpu.make_async_copy(grad.at[pl.ds(first, OWNED)], grad_v.at[j, r], load_sem.at[j, r, 1]))
        return found

    small = [
        pltpu.make_async_copy(src, dst, small_sem.at[i])
        for i, (src, dst) in enumerate(
            (
                (pin, pin_v), (pout, pout_v), (queries, q_v), (left, left_v), (right, right_v),
                (mask, mask_v), (lengths, len_s),
            )
        )
    ]
    small[0].start()
    small[1].start()
    for copy in loads(0):
        copy.start()
    for copy in small[2:]:
        copy.start()
    for j in range(1, AHEAD):
        for copy in loads(j):
            copy.start()

    barrier = pltpu.get_barrier_semaphore()
    greet = [(doc, place(*peer)) for peer in PEERS]
    greet += [(lax.rem(x + dx, 4) * 2 + hi, me) for dx in (1, 2, 3)]
    y_next = (x * 2 + 1 - hi, place(0, 1, 0))
    greet.append(y_next)
    for device in greet:
        pl.semaphore_signal(barrier, inc=1, device_id=device, device_id_type=MESH)

    small[0].wait()
    small[1].wait()
    r_, c_ = iota((RANK, RANK), 0), iota((RANK, RANK), 1)
    odd = (r_ >= 32).astype(jnp.int32)
    pick = jnp.where(c_ == 2 * (r_ - 32 * odd) + odd, 1.0, 0.0).astype(BF16)
    w_out[...] = dot(pick, pout_v[...]).astype(BF16)

    counter = [0]
    sent = []

    def send(src, dst, device):
        i = counter[0]
        counter[0] += 1
        copy = pltpu.make_async_remote_copy(
            src_ref=src, dst_ref=dst, send_sem=send_sem.at[i], recv_sem=recv_sem.at[i],
            device_id=device, device_id_type=MESH,
        )
        copy.start()
        sent.append(copy)
        return copy

    up, down = (doc, place(1, 0, 0)), (doc, place(3, 0, 0))
    twin_id, y_id = (doc, place(0, 0, 1)), (doc, place(0, 1, 0))
    core_copy, y_copy, z_copy = {}, {}, {}

    def project(j):
        for copy in loads(j):
            copy.wait()

        def one(i, carry):
            r = 1 - i
            a = jnp.concatenate([act_v[j, r, d] for d in range(OWNED)], axis=1)
            g = jnp.concatenate([grad_v[j, r, d] for d in range(OWNED)], axis=1)
            o_rows, i_rows = dot(w_out[...], g), dot(pin_v[...], a)
            for d in range(OWNED):
                blocks[j, r, d * SEQ : d * SEQ + RANK] = o_rows[:, d * SEQ : (d + 1) * SEQ]
                blocks[j, r, d * SEQ + RANK : (d + 1) * SEQ] = i_rows[:, d * SEQ : (d + 1) * SEQ]
            return carry

        lax.fori_loop(0, 2, one, 0)
        core_copy[j] = send(blocks.at[j, 1], twin.at[j], twin_id)

    def ref(t, dz, half):
        if t < 2:
            return blocks.at[PLACE[dz, t], 0, pl.ds(half * HALF_A, HALF_A)]
        return blocks.at[PLACE[dz, 1], 0, pl.ds(PART_A + half * HALF_B, HALF_B)]

    def far(t, half):
        return f_a.at[t, half] if t < 2 else f_b.at[half]

    def near(t, side, half):
        return n_a.at[t, side, half] if t < 2 else n_b.at[side, half]

    def send_far(t):
        z_copy[t, "f0"] = send(ref(t, 2, 0), far(t, 0), up)
        z_copy[t, "f1"] = send(ref(t, 2, 1), far(t, 1), down)

    def send_up_now(t):
        z_copy[t, "u1"] = send(ref(t, 1, 1), near(t, 0, 1), up)

    def send_down_now(t):
        z_copy[t, "d0"] = send(ref(t, 3, 0), near(t, 1, 0), down)

    def send_up_sum(t):
        z_copy[t, "f0"].wait_recv()
        ref(t, 1, 0)[...] += far(t, 0)[...]
        z_copy[t, "u0"] = send(ref(t, 1, 0), near(t, 0, 0), up)

    def send_down_sum(t):
        z_copy[t, "f1"].wait_recv()
        ref(t, 3, 1)[...] += far(t, 1)[...]
        z_copy[t, "d1"] = send(ref(t, 3, 1), near(t, 1, 1), down)

    def finish(t):
        for name in ("u1", "d0", "u0", "d1"):
            z_copy[t, name].wait_recv()
        for half in (0, 1):
            ref(t, 0, half)[...] += near(t, 0, half)[...] + near(t, 1, half)[...]

    def collect(j):
        dz, own = ORDER[j]
        core_copy[j].wait_recv()
        blocks[j, 0] += twin[j]
        if not own:
            y_copy[dz] = send(blocks.at[j, 0, pl.ds(PART_A, ROWS - PART_A)], y_b.at[dz], y_id)
        if dz == 2:
            send_far(own)
        elif dz == 1:
            send_up_now(own)
        elif dz == 3:
            send_down_now(own)

    def y_sum(dz):
        y_copy[dz].wait_recv()
        blocks[PLACE[dz, 1], 0, PART_A:ROWS] += y_b[dz]

    def precondition():
        for copy in small[2:5]:
            copy.wait()
        for m in range(32):
            t_own[m] = q_v[:, m * 128 : (m + 1) * 128]
        wide = jnp.where(lax.rem(iota((128, RANK), 0), RANK) == iota((128, RANK), 1), 1.0, 0.0)
        same = (iota((128, 128), 0) // RANK) == (iota((128, 128), 1) // RANK)
        both = dot(dot(wide, right_v[...], precision=HIGHEST), wide, (1, 1), precision=HIGHEST)
        both = jnp.where(same, both, 0.0)
        u = dot(t_own[...].reshape(256, 128), both, precision=HIGHEST)
        row, col = iota((256, RANK), 0), iota((256, RANK), 1)
        same_q = lax.rem(iota((256, 256), 0), 8) == lax.rem(iota((256, 256), 1), 8)
        take = [jnp.where(col == 2 * (row // 8) + e, 1.0, 0.0) for e in (0, 1)]
        lane = iota((256, 128), 1)
        halves = []
        for e_out in (0, 1):
            rows = dot(take[e_out], left_v[...], precision=HIGHEST)
            pieces = []
            for e_in in (0, 1):
                a = jnp.where(same_q, dot(rows, take[e_in], (1, 1), precision=HIGHEST), 0.0)
                pieces.append(dot(a, u, precision=HIGHEST))
            halves.append(pieces)
        low = halves[0][0] + pltpu.roll(halves[0][1], RANK, 1)
        high = pltpu.roll(halves[1][0], RANK, 1) + halves[1][1]
        t_own[...] = jnp.where(lane < RANK, low, high).reshape(32, 8, 128)

    t_copy = []

    def spread_queries():
        for peer in PEERS:
            param = place(*peer)
            t_copy.append(
                send(t_own.at[pl.ds(2 * part(param), 2)], t_all.at[:, doc, me], (doc, param))
            )
        mine = part(me)
        for m in (0, 1):
            t_all[m, doc, me] = t_own[2 * mine + m]

    def spread_y():
        for copy in t_copy:
            copy.wait_recv()
        return send(t_all.at[:, doc], t_all.at[:, doc], y_next)

    def spread_x(copy):
        copy.wait_recv()
        return [
            send(t_all.at[:, pl.ds(2 * x, 2)], t_all.at[:, pl.ds(2 * x, 2)], (lax.rem(x + dx, 4) * 2 + hi, me))
            for dx in (2, 1, 3)
        ]

    def chunk(j):
        if j + AHEAD < len(ORDER):
            for copy in loads(j + AHEAD):
                copy.start()
        if j == 0:
            pl.semaphore_wait(barrier, len(greet))
        project(j)

    chunk(0)
    chunk(1)
    collect(0)
    chunk(2)
    collect(1)
    precondition()
    spread_queries()
    collect(2)
    chunk(3)
    collect(3)
    chunk(4)
    send_up_sum(0)
    collect(4)
    send_down_sum(0)
    chunk(5)
    send_up_sum(1)
    collect(5)
    send_down_sum(1)
    y_sum(2)
    send_far(2)
    t_y = spread_y()
    chunk(6)
    collect(6)
    chunk(7)
    collect(7)
    y_sum(1)
    send_up_now(2)
    y_sum(3)
    send_down_now(2)
    t_x = spread_x(t_y)
    send_up_sum(2)
    send_down_sum(2)
    finish(0)
    last = send(blocks.at[PLACE[0, 0], 0, pl.ds(0, PART_A)], y_a, y_id)
    finish(1)
    for copy in t_x:
        copy.wait_recv()
    for m in (0, 1):
        high, low = split(t_all[m].reshape(1024, 128))
        t_high[:, m * 128 : (m + 1) * 128] = high
        t_low[:, m * 128 : (m + 1) * 128] = low
    y_sum(0)
    finish(2)
    last.wait_recv()
    home = PLACE[0, 1]
    blocks[home, 0, 0:PART_A] += y_a[...]

    for copy in small[5:]:
        copy.wait()
    lane = iota((32, 128), 1)
    for d in range(OWNED):
        row = me * OWNED + d
        weight = jnp.where(iota((1, SEQ), 1) < len_s[row], mask_v[pl.ds(row, 1), :].astype(F32), 0.0)
        o_rows = blocks[home, 0, d * SEQ : d * SEQ + RANK] * weight
        i_rows = blocks[home, 0, d * SEQ + RANK : (d + 1) * SEQ]
        prod = dot(jnp.concatenate(split(o_rows), axis=0), jnp.concatenate(split(i_rows), axis=0), (1, 1))
        prod = prod[:RANK] + prod[RANK:]
        prod = prod + pltpu.roll(prod, RANK, 1)
        whole = jnp.where(lane < RANK, prod[:32], prod[32:])
        for k in range(16):
            g_own[k, 2 * d : 2 * d + 2] = whole[2 * k : 2 * k + 2]

    g_copy = []
    for peer in PEERS:
        param = place(*peer)
        g_copy.append(send(g_own.at[part(param)], g_all.at[pl.ds(pl.multiple_of(me * 8, 8), 8)], (doc, param)))
    g_all[pl.ds(pl.multiple_of(me * 8, 8), 8), :] = g_own[part(me)]
    for copy in g_copy:
        copy.wait_recv()

    docs = jnp.concatenate([g_all[pl.ds(m, 64, stride=2), :] for m in (0, 1)], axis=1)
    high, low = split(docs)
    scores = dot(jnp.concatenate([high, low], axis=0), t_high[...], (1, 1))
    scores = scores[:64] + scores[64:] + dot(high, t_low[...], (1, 1))
    scores = scores * (1.0 / (RANK * SEQ**0.5))
    for k in range(16):
        s_own[k] = scores[OWNED * k : OWNED * (k + 1)]
    s_copy = []
    for peer in PEERS:
        param = place(*peer)
        s_copy.append(send(s_own.at[param], s_all.at[me], (doc, param)))
    s_all[me] = s_own[me]
    for copy in s_copy:
        copy.wait_recv()
    total = s_all[0]
    for k in range(1, 16):
        total = total + s_all[k]
    out[...] = total
    for copy in sent:
        copy.wait_send()


def body(activations, out_grads, proj_in, proj_out, lengths, loss_mask, queries, left_pre, right_pre):
    wide_in, wide_out = activations.shape[-1], out_grads.shape[-1]
    activations, out_grads = activations.transpose(0, 2, 1), out_grads.transpose(0, 2, 1)
    vmem = pltpu.VMEM
    return pl.pallas_call(
        kernel,
        out_shape=jax.ShapeDtypeStruct((OWNED, 1024), F32),
        in_specs=[pl.BlockSpec(memory_space=pl.ANY)] * 9,
        out_specs=pl.BlockSpec(memory_space=pltpu.VMEM),
        scratch_shapes=[
            vmem((8, 2, OWNED, wide_in, SEQ), BF16),
            vmem((8, 2, OWNED, wide_out, SEQ), BF16),
            vmem(proj_in.shape, BF16),
            vmem(proj_out.shape, BF16),
            pltpu.SMEM(lengths.shape, jnp.int32),
            vmem(loss_mask.shape, jnp.int32),
            vmem(queries.shape, F32),
            vmem(left_pre.shape, F32),
            vmem(right_pre.shape, F32),
            vmem(proj_out.shape, BF16),
            vmem((8, 2, ROWS, 128), F32),
            vmem((8, ROWS, 128), F32),
            vmem((2, 2, HALF_A, 128), F32),
            vmem((2, 2, 2, HALF_A, 128), F32),
            vmem((2, HALF_B, 128), F32),
            vmem((2, 2, HALF_B, 128), F32),
            vmem((PART_A, 128), F32),
            vmem((4, ROWS - PART_A, 128), F32),
            vmem((32, 8, 128), F32),
            vmem((2, 8, 16, 8, 128), F32),
            vmem((1024, 256), BF16),
            vmem((1024, 256), BF16),
            vmem((16, 8, 128), F32),
            vmem((128, 128), F32),
            vmem((16, OWNED, 1024), F32),
            vmem((16, OWNED, 1024), F32),
            pltpu.SemaphoreType.DMA((8, 2, 2)),
            pltpu.SemaphoreType.DMA((7,)),
            pltpu.SemaphoreType.DMA((N_SEMS,)),
            pltpu.SemaphoreType.DMA((N_SEMS,)),
        ],
        compiler_params=pltpu.CompilerParams(
            collective_id=0, has_side_effects=True, vmem_limit_bytes=60 * 1024 * 1024
        ),
        cost_estimate=pl.CostEstimate(flops=1_300_000_000, bytes_accessed=20_000_000, transcendentals=0),
    )(activations, out_grads, proj_in, proj_out, lengths, loss_mask, queries, left_pre, right_pre)


def solution(mesh):
    return jax.shard_map(
        body,
        mesh=mesh,
        in_specs=(
            P("doc", None, "param"),
            P("doc", None, "param"),
            P(None, "param"),
            P(None, "param"),
            P("doc"),
            P("doc", None),
            P(("doc", "param"), None),
            P(),
            P(),
        ),
        out_specs=P(("doc", "param"), None),
        check_vma=False,
    )
```

```python
import functools

import jax
import jax.numpy as jnp
from jax import lax
from jax.experimental import pallas as pl
from jax.experimental.pallas import tpu as pltpu
from jax.sharding import PartitionSpec as P

MESH = pl.DeviceIdType.MESH
F32 = jnp.float32
BF16 = jnp.bfloat16
HIGHEST = lax.Precision.HIGHEST

RANK = 64
SEQ = 128
OWNED = 4
ROWS = OWNED * SEQ
HALF_A = 144
HALF_B = 112
PART_A = 2 * HALF_A
AHEAD = 3
ORDER = ((2, 0), (2, 1), (1, 0), (3, 0), (1, 1), (3, 1), (0, 0), (0, 1))
PLACE = {step: j for j, step in enumerate(ORDER)}
PEERS = ((2, 1), (2, 0), (1, 1), (3, 1), (1, 0), (3, 0), (0, 1))
SLICE = 4
N_SEMS = 8 + 18 + 5 + 7 + 2 + 4 + 3 + 7 + 7


def iota(shape, dim):
    return lax.broadcasted_iota(jnp.int32, shape, dim)


def split(x):
    high = x.astype(BF16)
    return high, (x - high.astype(F32)).astype(BF16)


def dot(a, b, contract=(1, 0), precision=None):
    return lax.dot_general(
        a, b, (((contract[0],), (contract[1],)), ((), ())), precision=precision, preferred_element_type=F32
    )


def kernel(
    act, grad, pin, pout, lengths, mask, queries, left, right,
    out,
    act_v, grad_v, pin_v, pout_v, len_s, mask_v, q_v, left_v, right_v, w_out,
    blocks, twin, f_a, n_a, f_b, n_b, y_a, y_b,
    t_own, t_all, t_high, t_low, g_own, g_all, s_own, s_all,
    load_sem, small_sem, send_sem, recv_sem,
):
    doc, me = lax.axis_index("doc"), lax.axis_index("param")
    x, hi = doc // 2, lax.rem(doc, 2)
    z, lo, core = me // 4, lax.rem(me // 2, 2), lax.rem(me, 2)

    def place(dz, dy, dc):
        py = 1 - lo if dy else lo
        pc = 1 - core if dc else core
        return lax.rem(z + dz, 4) * 4 + py * 2 + pc

    def part(dz, dy):
        py = 1 - lo if dy else lo
        return lax.rem(z + dz, 4) * 2 + py + hi - 2 * py * hi

    def loads(j):
        dz, own = ORDER[j]
        found = []
        for r in (1, 0):
            first = place(dz, 1 - own, r) * OWNED
            found.append(pltpu.make_async_copy(act.at[pl.ds(first, OWNED)], act_v.at[j, r], load_sem.at[j, r, 0]))
            found.append(pltpu.make_async_copy(grad.at[pl.ds(first, OWNED)], grad_v.at[j, r], load_sem.at[j, r, 1]))
        return found

    small = [
        pltpu.make_async_copy(src, dst, small_sem.at[i])
        for i, (src, dst) in enumerate(
            (
                (pin, pin_v), (pout, pout_v), (queries, q_v), (left, left_v), (right, right_v),
                (mask, mask_v), (lengths, len_s),
            )
        )
    ]
    for copy in small[:5]:
        copy.start()
    for copy in loads(0):
        copy.start()
    for copy in small[5:]:
        copy.start()
    for j in range(1, AHEAD):
        for copy in loads(j):
            copy.start()

    barrier = pltpu.get_barrier_semaphore()
    greet = [(doc, place(*peer, 0)) for peer in PEERS] + [(doc, place(0, 0, 1))]
    greet += [(lax.rem(x + dx, 4) * 2 + hi, me) for dx in (1, 2, 3)]
    y_next = (x * 2 + 1 - hi, place(0, 1, 0))
    greet.append(y_next)
    for device in greet:
        pl.semaphore_signal(barrier, inc=1, device_id=device, device_id_type=MESH)

    small[0].wait()
    small[1].wait()
    r_, c_ = iota((RANK, RANK), 0), iota((RANK, RANK), 1)
    odd = (r_ >= 32).astype(jnp.int32)
    pick = jnp.where(c_ == 2 * (r_ - 32 * odd) + odd, 1.0, 0.0).astype(BF16)
    w_out[...] = dot(pick, pout_v[...]).astype(BF16)

    counter = [0]
    sent = []

    def send(src, dst, device):
        i = counter[0]
        counter[0] += 1
        copy = pltpu.make_async_remote_copy(
            src_ref=src, dst_ref=dst, send_sem=send_sem.at[i], recv_sem=recv_sem.at[i],
            device_id=device, device_id_type=MESH,
        )
        copy.start()
        sent.append(copy)
        return copy

    up, down = (doc, place(1, 0, 0)), (doc, place(3, 0, 0))
    twin_id, y_id = (doc, place(0, 0, 1)), (doc, place(0, 1, 0))
    core_copy, y_copy, z_copy = {}, {}, {}

    def project(j):
        for copy in loads(j):
            copy.wait()

        def one(i, carry):
            r = 1 - i
            a = jnp.concatenate([act_v[j, r, d] for d in range(OWNED)], axis=1)
            g = jnp.concatenate([grad_v[j, r, d] for d in range(OWNED)], axis=1)
            o_rows, i_rows = dot(w_out[...], g), dot(pin_v[...], a)
            for d in range(OWNED):
                blocks[j, r, d * SEQ : d * SEQ + RANK] = o_rows[:, d * SEQ : (d + 1) * SEQ]
                blocks[j, r, d * SEQ + RANK : (d + 1) * SEQ] = i_rows[:, d * SEQ : (d + 1) * SEQ]
            return carry

        lax.fori_loop(0, 2, one, 0)
        core_copy[j] = send(blocks.at[j, 1], twin.at[j], twin_id)

    def ref(t, dz, half):
        if t < 2:
            return blocks.at[PLACE[dz, t], 0, pl.ds(half * HALF_A, HALF_A)]
        return blocks.at[PLACE[dz, 1], 0, pl.ds(PART_A + half * HALF_B, HALF_B)]

    def far(t, half):
        return f_a.at[t, half] if t < 2 else f_b.at[half]

    def near(t, side, half):
        return n_a.at[t, side, half] if t < 2 else n_b.at[side, half]

    def send_far(t):
        z_copy[t, "f0"] = send(ref(t, 2, 0), far(t, 0), up)
        z_copy[t, "f1"] = send(ref(t, 2, 1), far(t, 1), down)

    def send_up_now(t):
        z_copy[t, "u1"] = send(ref(t, 1, 1), near(t, 0, 1), up)

    def send_down_now(t):
        z_copy[t, "d0"] = send(ref(t, 3, 0), near(t, 1, 0), down)

    def send_up_sum(t):
        z_copy[t, "f0"].wait_recv()
        ref(t, 1, 0)[...] += far(t, 0)[...]
        z_copy[t, "u0"] = send(ref(t, 1, 0), near(t, 0, 0), up)

    def send_down_sum(t):
        z_copy[t, "f1"].wait_recv()
        ref(t, 3, 1)[...] += far(t, 1)[...]
        z_copy[t, "d1"] = send(ref(t, 3, 1), near(t, 1, 1), down)

    def finish(t):
        for name in ("u1", "d0", "u0", "d1"):
            z_copy[t, name].wait_recv()
        for half in (0, 1):
            ref(t, 0, half)[...] += near(t, 0, half)[...] + near(t, 1, half)[...]

    def collect(j):
        dz, own = ORDER[j]
        core_copy[j].wait_recv()
        blocks[j, 0] += twin[j]
        if not own:
            y_copy[dz] = send(blocks.at[j, 0, pl.ds(PART_A, ROWS - PART_A)], y_b.at[dz], y_id)
        if dz == 2:
            send_far(own)
        elif dz == 1:
            send_up_now(own)
        elif dz == 3:
            send_down_now(own)

    def y_sum(dz):
        y_copy[dz].wait_recv()
        blocks[PLACE[dz, 1], 0, PART_A:ROWS] += y_b[dz]

    def precondition():
        for copy in small[2:5]:
            copy.wait()
        pick32 = pick.astype(F32)
        l_perm = dot(dot(pick32, left_v[...], precision=HIGHEST), pick32, (1, 1), precision=HIGHEST)
        none = jnp.zeros((RANK, RANK), F32)
        r_twice = jnp.concatenate(
            [jnp.concatenate([right_v[...], none], axis=1), jnp.concatenate([none, right_v[...]], axis=1)], axis=0
        )
        rows = jnp.concatenate([q_v[:, m * 128 : (m + 1) * 128] for m in range(32)], axis=0)
        t_own[...] = dot(rows, r_twice, precision=HIGHEST).reshape(32, 8, 128)
        lane = iota((32, 128), 1) < RANK

        def pair(a, b):
            return jnp.where(lane, a, pltpu.roll(b, RANK, 1)), jnp.where(lane, pltpu.roll(a, RANK, 1), b)

        pairs = [pair(t_own[:, 2 * i], t_own[:, 2 * i + 1]) for i in range(4)]
        cols = jnp.concatenate([jnp.concatenate(p, axis=0) for p in pairs], axis=1)
        cols = dot(l_perm, cols, precision=HIGHEST)
        for i in range(4):
            a, b = pair(cols[:32, i * 128 : (i + 1) * 128], cols[32:, i * 128 : (i + 1) * 128])
            t_own[:, 2 * i] = a
            t_own[:, 2 * i + 1] = b

    slot = me // 2
    t_copy, t_twin = [], []

    def share(first, count):
        block = t_all.at[:, core, pl.ds(first, count)]
        t_twin.append(send(block, block, twin_id))

    def spread_queries():
        for peer in PEERS:
            t_copy.append(
                send(
                    t_own.at[pl.ds(SLICE * part(*peer), SLICE)], t_all.at[:, core, doc, slot], (doc, place(*peer, 0))
                )
            )
        mine = part(0, 0)
        for m in range(SLICE):
            t_all[m, core, doc, slot] = t_own[SLICE * mine + m]

    def spread_y():
        for copy in t_copy:
            copy.wait_recv()
        t_copy.append(send(t_all.at[:, core, doc], t_all.at[:, core, doc], y_next))

    def spread_x():
        t_copy.pop().wait_recv()
        t_copy.clear()
        block = t_all.at[:, core, pl.ds(2 * x, 2)]
        for dx in (2, 1, 3):
            t_copy.append(send(block, block, (lax.rem(x + dx, 4) * 2 + hi, me)))
        share(2 * x, 2)

    def spread_twin():
        for dx, copy in zip((1, 3, 2), (t_copy[1], t_copy[2], t_copy[0])):
            copy.wait_recv()
            share(2 * lax.rem(x + 4 - dx, 4), 2)

    def chunk(j):
        if j + AHEAD < len(ORDER):
            for copy in loads(j + AHEAD):
                copy.start()
        project(j)

    precondition()
    pl.semaphore_wait(barrier, len(greet))
    spread_queries()
    chunk(0)
    chunk(1)
    collect(0)
    chunk(2)
    collect(1)
    chunk(3)
    collect(2)
    spread_y()
    chunk(4)
    collect(3)
    send_up_sum(0)
    chunk(5)
    collect(4)
    send_down_sum(0)
    chunk(6)
    collect(5)
    send_up_sum(1)
    send_down_sum(1)
    chunk(7)
    collect(6)
    y_sum(2)
    send_far(2)
    collect(7)
    spread_x()
    y_sum(1)
    send_up_now(2)
    y_sum(3)
    send_down_now(2)
    finish(0)
    last = send(blocks.at[PLACE[0, 0], 0, pl.ds(0, PART_A)], y_a, y_id)
    send_up_sum(2)
    send_down_sum(2)
    finish(1)
    y_sum(0)
    finish(2)
    last.wait_recv()
    home = PLACE[0, 1]
    blocks[home, 0, 0:PART_A] += y_a[...]

    for copy in small[5:]:
        copy.wait()
    lane = iota((32, 128), 1)
    for d in range(OWNED):
        row = me * OWNED + d
        weight = jnp.where(iota((1, SEQ), 1) < len_s[row], mask_v[pl.ds(row, 1), :].astype(F32), 0.0)
        o_rows = blocks[home, 0, d * SEQ : d * SEQ + RANK] * weight
        i_rows = blocks[home, 0, d * SEQ + RANK : (d + 1) * SEQ]
        prod = dot(jnp.concatenate(split(o_rows), axis=0), jnp.concatenate(split(i_rows), axis=0), (1, 1))
        prod = prod[:RANK] + prod[RANK:]
        prod = prod + pltpu.roll(prod, RANK, 1)
        whole = jnp.where(lane < RANK, prod[:32], prod[32:])
        for k in range(8):
            g_own[k, SLICE * d : SLICE * (d + 1)] = whole[SLICE * k : SLICE * (k + 1)]

    g_copy = []
    mine = pl.ds(pl.multiple_of(slot * 16, 16), 16)
    for peer in PEERS:
        g_copy.append(send(g_own.at[part(*peer)], g_all.at[mine], (doc, place(*peer, 0))))
    g_all[mine, :] = g_own[part(0, 0)]

    spread_twin()
    for copy in t_twin:
        copy.wait_recv()
    for m in range(SLICE):
        rows = jnp.stack([t_all[m, c].reshape(RANK, 8, 128) for c in (0, 1)], axis=1).reshape(1024, 128)
        high, low = split(rows)
        t_high[:, m * 128 : (m + 1) * 128] = high
        t_low[:, m * 128 : (m + 1) * 128] = low
    for copy in g_copy:
        copy.wait_recv()

    docs = jnp.concatenate([g_all[pl.ds(m, 32, stride=SLICE), :] for m in range(SLICE)], axis=1)
    high, low = split(docs)
    scores = dot(jnp.concatenate([high, low], axis=0), t_high[...], (1, 1))
    scores = scores[:32] + scores[32:] + dot(high, t_low[...], (1, 1))
    scores = scores * (1.0 / (RANK * SEQ**0.5))
    for k in range(8):
        s_own[k] = scores[OWNED * k : OWNED * (k + 1)]
    s_copy = []
    for dz, dy in PEERS:
        param = place(dz, dy, 0)
        s_copy.append(send(s_own.at[param // 2], s_all.at[slot], (doc, param)))
    s_all[slot] = s_own[slot]
    for copy in s_copy:
        copy.wait_recv()
    total = s_all[0]
    for k in range(1, 8):
        total = total + s_all[k]
    out[...] = total
    for copy in sent:
        copy.wait_send()


def body(activations, out_grads, proj_in, proj_out, lengths, loss_mask, queries, left_pre, right_pre):
    wide_in, wide_out = activations.shape[-1], out_grads.shape[-1]
    activations, out_grads = activations.transpose(0, 2, 1), out_grads.transpose(0, 2, 1)
    vmem = pltpu.VMEM
    return pl.pallas_call(
        kernel,
        out_shape=jax.ShapeDtypeStruct((OWNED, 1024), F32),
        in_specs=[pl.BlockSpec(memory_space=pl.ANY)] * 9,
        out_specs=pl.BlockSpec(memory_space=pltpu.VMEM),
        scratch_shapes=[
            vmem((8, 2, OWNED, wide_in, SEQ), BF16),
            vmem((8, 2, OWNED, wide_out, SEQ), BF16),
            vmem(proj_in.shape, BF16),
            vmem(proj_out.shape, BF16),
            pltpu.SMEM(lengths.shape, jnp.int32),
            vmem(loss_mask.shape, jnp.int32),
            vmem(queries.shape, F32),
            vmem(left_pre.shape, F32),
            vmem(right_pre.shape, F32),
            vmem(proj_out.shape, BF16),
            vmem((8, 2, ROWS, 128), F32),
            vmem((8, ROWS, 128), F32),
            vmem((2, 2, HALF_A, 128), F32),
            vmem((2, 2, 2, HALF_A, 128), F32),
            vmem((2, HALF_B, 128), F32),
            vmem((2, 2, HALF_B, 128), F32),
            vmem((PART_A, 128), F32),
            vmem((4, ROWS - PART_A, 128), F32),
            vmem((32, 8, 128), F32),
            vmem((SLICE, 2, 8, 8, 8, 128), F32),
            vmem((1024, SLICE * 128), BF16),
            vmem((1024, SLICE * 128), BF16),
            vmem((8, SLICE * OWNED, 128), F32),
            vmem((128, 128), F32),
            vmem((8, OWNED, 1024), F32),
            vmem((8, OWNED, 1024), F32),
            pltpu.SemaphoreType.DMA((8, 2, 2)),
            pltpu.SemaphoreType.DMA((7,)),
            pltpu.SemaphoreType.DMA((N_SEMS,)),
            pltpu.SemaphoreType.DMA((N_SEMS,)),
        ],
        compiler_params=pltpu.CompilerParams(
            collective_id=0, has_side_effects=True, vmem_limit_bytes=60 * 1024 * 1024
        ),
        cost_estimate=pl.CostEstimate(flops=1_300_000_000, bytes_accessed=20_000_000, transcendentals=0),
    )(activations, out_grads, proj_in, proj_out, lengths, loss_mask, queries, left_pre, right_pre)


def solution(mesh):
    return jax.shard_map(
        body,
        mesh=mesh,
        in_specs=(
            P("doc", None, "param"),
            P("doc", None, "param"),
            P(None, "param"),
            P(None, "param"),
            P("doc"),
            P("doc", None),
            P(("doc", "param"), None),
            P(),
            P(),
        ),
        out_specs=P(("doc", "param"), None),
        check_vma=False,
    )
```

```python
import functools

import jax
import jax.numpy as jnp
from jax import lax
from jax.experimental import pallas as pl
from jax.experimental.pallas import tpu as pltpu
from jax.sharding import PartitionSpec as P

MESH = pl.DeviceIdType.MESH
F32 = jnp.float32
BF16 = jnp.bfloat16
HIGHEST = lax.Precision.HIGHEST

RANK = 64
SEQ = 128
OWNED = 4
ROWS = OWNED * SEQ
HALF_A = 144
HALF_B = 112
PART_A = 2 * HALF_A
AHEAD = 3
ORDER = ((2, 0), (2, 1), (1, 0), (3, 0), (1, 1), (3, 1), (0, 0), (0, 1))
PLACE = {step: j for j, step in enumerate(ORDER)}
PEERS = ((2, 1), (2, 0), (1, 1), (3, 1), (1, 0), (3, 0), (0, 1))
SLICE = 4
WIDE = SLICE * 128
N_SEMS = 8 + 18 + 5 + 7 + 2 + 5 + 8 + 7 + 7


def iota(shape, dim):
    return lax.broadcasted_iota(jnp.int32, shape, dim)


def split(x):
    high = x.astype(BF16)
    return high, (x - high.astype(F32)).astype(BF16)


def dot(a, b, contract=(1, 0), precision=None):
    return lax.dot_general(
        a, b, (((contract[0],), (contract[1],)), ((), ())), precision=precision, preferred_element_type=F32
    )


def kernel(
    act, grad, pin, pout, lengths, mask, queries, left, right,
    out,
    act_v, grad_v, pin_v, pout_v, len_s, mask_v, left_v, right_v,
    blocks, twin, f_a, n_a, f_b, n_b, y_a, y_b,
    t_all, t_high, t_low, g_own, g_all, s_own, s_all,
    load_sem, small_sem, send_sem, recv_sem,
):
    doc, me = lax.axis_index("doc"), lax.axis_index("param")
    x, hi = doc // 2, lax.rem(doc, 2)
    z, lo, core = me // 4, lax.rem(me // 2, 2), lax.rem(me, 2)

    def place(dz, dy, dc):
        py = 1 - lo if dy else lo
        pc = 1 - core if dc else core
        return lax.rem(z + dz, 4) * 4 + py * 2 + pc

    def part(dz, dy):
        py = 1 - lo if dy else lo
        return lax.rem(z + dz, 4) * 2 + py + hi - 2 * py * hi

    def loads(j):
        dz, own = ORDER[j]
        found = []
        for r in (1, 0):
            first = place(dz, 1 - own, r) * OWNED
            found.append(pltpu.make_async_copy(act.at[pl.ds(first, OWNED)], act_v.at[j, r], load_sem.at[j, r, 0]))
            found.append(pltpu.make_async_copy(grad.at[pl.ds(first, OWNED)], grad_v.at[j, r], load_sem.at[j, r, 1]))
        return found

    small = [
        pltpu.make_async_copy(src, dst, small_sem.at[i])
        for i, (src, dst) in enumerate(
            (
                (pout, pout_v), (pin, pin_v), (left, left_v), (right, right_v), (mask, mask_v), (lengths, len_s),
            )
        )
    ]
    for copy in small[:2]:
        copy.start()
    for copy in loads(0):
        copy.start()
    for copy in small[2:]:
        copy.start()
    for j in range(1, AHEAD):
        for copy in loads(j):
            copy.start()

    barrier = pltpu.get_barrier_semaphore()
    greet = [(doc, place(*peer, 0)) for peer in PEERS] + [(doc, place(0, 0, 1))]
    greet += [(lax.rem(x + dx, 4) * 2 + hi, me) for dx in (1, 2, 3)]
    y_next = (x * 2 + 1 - hi, place(0, 1, 0))
    greet.append(y_next)
    for device in greet:
        pl.semaphore_signal(barrier, inc=1, device_id=device, device_id_type=MESH)

    counter = [0]
    sent = []

    def send(src, dst, device):
        i = counter[0]
        counter[0] += 1
        copy = pltpu.make_async_remote_copy(
            src_ref=src, dst_ref=dst, send_sem=send_sem.at[i], recv_sem=recv_sem.at[i],
            device_id=device, device_id_type=MESH,
        )
        copy.start()
        sent.append(copy)
        return copy

    up, down = (doc, place(1, 0, 0)), (doc, place(3, 0, 0))
    twin_id, y_id = (doc, place(0, 0, 1)), (doc, place(0, 1, 0))
    core_copy, y_copy, z_copy = {}, {}, {}

    def project(j):
        copies = loads(j)

        def one(r):
            for copy in copies[:2] if r else copies[2:]:
                copy.wait()
            a = jnp.concatenate([act_v[j, r, d] for d in range(OWNED)], axis=1)
            g = jnp.concatenate([grad_v[j, r, d] for d in range(OWNED)], axis=1)
            o_rows, i_rows = dot(pout_v[...], g), dot(pin_v[...], a)
            for d in range(OWNED):
                blocks[j, r, d * SEQ : d * SEQ + RANK] = o_rows[:, d * SEQ : (d + 1) * SEQ]
                blocks[j, r, d * SEQ + RANK : (d + 1) * SEQ] = i_rows[:, d * SEQ : (d + 1) * SEQ]

        one(1)
        core_copy[j] = send(blocks.at[j, 1], twin.at[j], twin_id)
        one(0)

    def ref(t, dz, half):
        if t < 2:
            return blocks.at[PLACE[dz, t], 0, pl.ds(half * HALF_A, HALF_A)]
        return blocks.at[PLACE[dz, 1], 0, pl.ds(PART_A + half * HALF_B, HALF_B)]

    def far(t, half):
        return f_a.at[t, half] if t < 2 else f_b.at[half]

    def near(t, side, half):
        return n_a.at[t, side, half] if t < 2 else n_b.at[side, half]

    def send_far(t):
        z_copy[t, "f0"] = send(ref(t, 2, 0), far(t, 0), up)
        z_copy[t, "f1"] = send(ref(t, 2, 1), far(t, 1), down)

    def send_up_now(t):
        z_copy[t, "u1"] = send(ref(t, 1, 1), near(t, 0, 1), up)

    def send_down_now(t):
        z_copy[t, "d0"] = send(ref(t, 3, 0), near(t, 1, 0), down)

    def send_up_sum(t):
        z_copy[t, "f0"].wait_recv()
        ref(t, 1, 0)[...] += far(t, 0)[...]
        z_copy[t, "u0"] = send(ref(t, 1, 0), near(t, 0, 0), up)

    def send_down_sum(t):
        z_copy[t, "f1"].wait_recv()
        ref(t, 3, 1)[...] += far(t, 1)[...]
        z_copy[t, "d1"] = send(ref(t, 3, 1), near(t, 1, 1), down)

    def finish(t):
        for name in ("u1", "d0", "u0", "d1"):
            z_copy[t, name].wait_recv()
        for half in (0, 1):
            ref(t, 0, half)[...] += near(t, 0, half)[...] + near(t, 1, half)[...]

    def collect(j):
        dz, own = ORDER[j]
        core_copy[j].wait_recv()
        blocks[j, 0] += twin[j]
        if not own:
            y_copy[dz] = send(blocks.at[j, 0, pl.ds(PART_A, ROWS - PART_A)], y_b.at[dz], y_id)
        if dz == 2:
            send_far(own)
        elif dz == 1:
            send_up_now(own)
        elif dz == 3:
            send_down_now(own)

    def y_sum(dz):
        y_copy[dz].wait_recv()
        blocks[PLACE[dz, 1], 0, PART_A:ROWS] += y_b[dz]

    slot = me // 2
    t_copy, t_twin, t_y, t_x = [], [], [], {}

    def piece(k):
        return queries.at[:, pl.ds(pl.multiple_of(WIDE * k, WIDE), WIDE)]

    own_piece = pltpu.make_async_copy(piece(part(0, 0)), t_all.at[core, doc, slot], small_sem.at[len(small)])

    def spread(g, device):
        block = t_all.at[core, g]
        return send(block, block, device)

    def share(g):
        t_twin.append(spread(g, twin_id))

    def x_id(dx):
        return (lax.rem(x + dx, 4) * 2 + hi, me)

    def x_doc(dx, half):
        return 2 * lax.rem(x + 4 - dx, 4) + (1 - hi if half else hi)

    def spread_queries():
        own_piece.start()
        for peer in PEERS:
            t_copy.append(send(piece(part(*peer)), t_all.at[core, doc, slot], (doc, place(*peer, 0))))

    def spread_own():
        own_piece.wait()
        for copy in t_copy:
            copy.wait_recv()
        t_y.append(spread(doc, y_next))
        for dx in (2, 1, 3):
            t_x[dx, 0] = spread(doc, x_id(dx))
        share(doc)

    def spread_other():
        t_y[0].wait_recv()
        for dx in (1, 3):
            t_x[dx, 1] = spread(x_doc(0, 1), x_id(dx))
        share(x_doc(0, 1))

    def spread_far():
        t_x[2, 0].wait_recv()
        t_y.append(spread(x_doc(2, 0), y_next))
        share(x_doc(2, 0))

    def spread_twin(half):
        for dx in (1, 3):
            t_x[dx, half].wait_recv()
            share(x_doc(dx, half))

    def spread_last():
        spread_twin(1)
        t_y[1].wait_recv()
        share(x_doc(2, 1))

    def chunk(j):
        if j + AHEAD < len(ORDER):
            for copy in loads(j + AHEAD):
                copy.start()
        project(j)

    pl.semaphore_wait(barrier, len(greet))
    spread_queries()
    for copy in small[:2]:
        copy.wait()
    chunk(0)
    chunk(1)
    collect(0)
    chunk(2)
    collect(1)
    chunk(3)
    collect(2)
    spread_own()
    chunk(4)
    collect(3)
    send_up_sum(0)
    chunk(5)
    collect(4)
    send_down_sum(0)
    y_sum(2)
    send_far(2)
    chunk(6)
    collect(5)
    send_up_sum(1)
    send_down_sum(1)
    chunk(7)
    collect(6)
    collect(7)
    spread_other()
    y_sum(1)
    send_up_now(2)
    finish(0)
    last = send(blocks.at[PLACE[0, 0], 0, pl.ds(0, PART_A)], y_a, y_id)
    spread_far()
    y_sum(3)
    send_down_now(2)
    spread_twin(0)
    send_up_sum(2)
    send_down_sum(2)
    finish(1)
    for copy in small[2:]:
        copy.wait()
    r_, c_ = iota((RANK, RANK), 0), iota((RANK, RANK), 1)
    odd = (r_ >= 32).astype(jnp.int32)
    pick = jnp.where(c_ == 2 * (r_ - 32 * odd) + odd, 1.0, 0.0)
    none = jnp.zeros((RANK, RANK), F32)
    p_high, p_low = split(
        jnp.concatenate(
            [
                jnp.concatenate([dot(pick, left_v[...], (1, 1), precision=HIGHEST), none], axis=1),
                jnp.concatenate([none, right_v[...]], axis=1),
            ],
            axis=0,
        )
    )
    home = PLACE[0, 1]
    lane = iota((32, 128), 1)

    def gradients(docs):
        cols = jnp.concatenate([blocks[home, 0, d * SEQ : (d + 1) * SEQ] for d in docs], axis=1)
        high, low = split(cols)
        cols = dot(p_high, high) + (dot(p_high, low) + dot(p_low, high))
        for i, d in enumerate(docs):
            row = me * OWNED + d
            weight = jnp.where(iota((1, SEQ), 1) < len_s[row], mask_v[pl.ds(row, 1), :].astype(F32), 0.0)
            o_rows = cols[:RANK, i * SEQ : (i + 1) * SEQ] * weight
            i_rows = cols[RANK:, i * SEQ : (i + 1) * SEQ]
            prod = dot(jnp.concatenate(split(o_rows), axis=0), jnp.concatenate(split(i_rows), axis=0), (1, 1))
            prod = prod[:RANK] + prod[RANK:]
            prod = prod + pltpu.roll(prod, RANK, 1)
            whole = jnp.where(lane < RANK, prod[:32], prod[32:])
            for k in range(8):
                g_own[k, SLICE * d : SLICE * (d + 1)] = whole[SLICE * k : SLICE * (k + 1)]

    last.wait_recv()
    blocks[home, 0, 0:PART_A] += y_a[...]
    gradients((0, 1))
    y_sum(0)
    finish(2)
    gradients((2, 3))

    g_copy = []
    mine = pl.ds(pl.multiple_of(slot * 16, 16), 16)
    for peer in PEERS:
        g_copy.append(send(g_own.at[part(*peer)], g_all.at[mine], (doc, place(*peer, 0))))
    g_all[mine, :] = g_own[part(0, 0)]

    spread_last()
    for copy in t_twin:
        copy.wait_recv()
    rows = jnp.stack([t_all[c].reshape(RANK, 8, WIDE) for c in (0, 1)], axis=1).reshape(1024, WIDE)
    t_high[...], t_low[...] = split(rows)
    early = [copy for copy in sent if not any(copy is other for other in g_copy)]
    for copy in early:
        copy.wait_send()
    for copy in g_copy:
        copy.wait_recv()

    docs = jnp.concatenate([g_all[pl.ds(m, 32, stride=SLICE), :] for m in range(SLICE)], axis=1)
    high, low = split(docs)
    scores = dot(jnp.concatenate([high, low], axis=0), t_high[...], (1, 1))
    scores = scores[:32] + scores[32:] + dot(high, t_low[...], (1, 1))
    scores = scores * (1.0 / (RANK * SEQ**0.5))
    for k in range(8):
        s_own[k] = scores[OWNED * k : OWNED * (k + 1)]
    s_copy = []
    for dz, dy in PEERS:
        param = place(dz, dy, 0)
        s_copy.append(send(s_own.at[param // 2], s_all.at[slot], (doc, param)))
    s_all[slot] = s_own[slot]
    for copy in s_copy:
        copy.wait_recv()
    total = s_all[0]
    for k in range(1, 8):
        total = total + s_all[k]
    out[...] = total
    for copy in g_copy + s_copy:
        copy.wait_send()


def body(activations, out_grads, proj_in, proj_out, lengths, loss_mask, queries, left_pre, right_pre):
    wide_in, wide_out = activations.shape[-1], out_grads.shape[-1]
    activations, out_grads = activations.transpose(0, 2, 1), out_grads.transpose(0, 2, 1)
    vmem = pltpu.VMEM
    return pl.pallas_call(
        kernel,
        out_shape=jax.ShapeDtypeStruct((OWNED, 1024), F32),
        in_specs=[pl.BlockSpec(memory_space=pl.ANY)] * 9,
        out_specs=pl.BlockSpec(memory_space=pltpu.VMEM),
        scratch_shapes=[
            vmem((8, 2, OWNED, wide_in, SEQ), BF16),
            vmem((8, 2, OWNED, wide_out, SEQ), BF16),
            vmem(proj_in.shape, BF16),
            vmem(proj_out.shape, BF16),
            pltpu.SMEM(lengths.shape, jnp.int32),
            vmem(loss_mask.shape, jnp.int32),
            vmem(left_pre.shape, F32),
            vmem(right_pre.shape, F32),
            vmem((8, 2, ROWS, 128), F32),
            vmem((8, ROWS, 128), F32),
            vmem((2, 2, HALF_A, 128), F32),
            vmem((2, 2, 2, HALF_A, 128), F32),
            vmem((2, HALF_B, 128), F32),
            vmem((2, 2, HALF_B, 128), F32),
            vmem((PART_A, 128), F32),
            vmem((4, ROWS - PART_A, 128), F32),
            vmem((2, 8, 8, 8, WIDE), F32),
            vmem((1024, WIDE), BF16),
            vmem((1024, WIDE), BF16),
            vmem((8, SLICE * OWNED, 128), F32),
            vmem((128, 128), F32),
            vmem((8, OWNED, 1024), F32),
            vmem((8, OWNED, 1024), F32),
            pltpu.SemaphoreType.DMA((8, 2, 2)),
            pltpu.SemaphoreType.DMA((7,)),
            pltpu.SemaphoreType.DMA((N_SEMS,)),
            pltpu.SemaphoreType.DMA((N_SEMS,)),
        ],
        compiler_params=pltpu.CompilerParams(
            collective_id=0, has_side_effects=True, vmem_limit_bytes=60 * 1024 * 1024
        ),
        cost_estimate=pl.CostEstimate(flops=1_300_000_000, bytes_accessed=20_000_000, transcendentals=0),
    )(activations, out_grads, proj_in, proj_out, lengths, loss_mask, queries, left_pre, right_pre)


def solution(mesh):
    return jax.shard_map(
        body,
        mesh=mesh,
        in_specs=(
            P("doc", None, "param"),
            P("doc", None, "param"),
            P(None, "param"),
            P(None, "param"),
            P("doc"),
            P("doc", None),
            P(("doc", "param"), None),
            P(),
            P(),
        ),
        out_specs=P(("doc", "param"), None),
        check_vma=False,
    )
```

```python
import functools

import jax
import jax.numpy as jnp
from jax import lax
from jax.experimental import pallas as pl
from jax.experimental.pallas import tpu as pltpu
from jax.sharding import PartitionSpec as P

MESH = pl.DeviceIdType.MESH
F32 = jnp.float32
BF16 = jnp.bfloat16
HIGHEST = lax.Precision.HIGHEST

RANK = 64
SEQ = 128
OWNED = 4
ROWS = OWNED * SEQ
HALF_A = 144
HALF_B = 112
PART_A = 2 * HALF_A
AHEAD = 3
ORDER = ((2, 0), (2, 1), (1, 0), (3, 0), (1, 1), (3, 1), (0, 0), (0, 1))
PLACE = {step: j for j, step in enumerate(ORDER)}
PEERS = ((2, 1), (2, 0), (1, 1), (3, 1), (1, 0), (3, 0), (0, 1))
SLICE = 4
WIDE = SLICE * 128
N_SEMS = 8 + 18 + 5 + 7 + 2 + 5 + 8 + 7 + 7


def iota(shape, dim):
    return lax.broadcasted_iota(jnp.int32, shape, dim)


def split(x):
    high = x.astype(BF16)
    return high, (x - high.astype(F32)).astype(BF16)


def dot(a, b, contract=(1, 0), precision=None):
    return lax.dot_general(
        a, b, (((contract[0],), (contract[1],)), ((), ())), precision=precision, preferred_element_type=F32
    )


def kernel(
    act, grad, pin, pout, lengths, mask, queries, left, right,
    out,
    act_v, grad_v, pin_v, pout_v, len_s, mask_v, left_v, right_v,
    blocks, twin, f_a, n_a, f_b, n_b, y_a, y_b,
    t_all, t_high, t_low, g_own, g_all, s_own, s_all,
    load_sem, small_sem, send_sem, recv_sem,
):
    doc, me = lax.axis_index("doc"), lax.axis_index("param")
    x, hi = doc // 2, lax.rem(doc, 2)
    z, lo, core = me // 4, lax.rem(me // 2, 2), lax.rem(me, 2)

    def place(dz, dy, dc):
        py = 1 - lo if dy else lo
        pc = 1 - core if dc else core
        return lax.rem(z + dz, 4) * 4 + py * 2 + pc

    def part(dz, dy):
        py = 1 - lo if dy else lo
        return lax.rem(z + dz, 4) * 2 + py + hi - 2 * py * hi

    def loads(j):
        dz, own = ORDER[j]
        first = place(dz, 1 - own, 0) // 2 * 2 * OWNED
        found = [
            pltpu.make_async_copy(act.at[pl.ds(first, 2 * OWNED)], act_v.at[j], load_sem.at[j, 0]),
            pltpu.make_async_copy(grad.at[pl.ds(first, 2 * OWNED)], grad_v.at[j], load_sem.at[j, 1]),
        ]
        return found

    small = [
        pltpu.make_async_copy(src, dst, small_sem.at[i])
        for i, (src, dst) in enumerate(
            (
                (pout, pout_v), (pin, pin_v), (left, left_v), (right, right_v), (mask, mask_v), (lengths, len_s),
            )
        )
    ]
    for copy in small[:2]:
        copy.start()
    for copy in loads(0):
        copy.start()
    for copy in small[2:]:
        copy.start()
    for j in range(1, AHEAD):
        for copy in loads(j):
            copy.start()

    barrier = pltpu.get_barrier_semaphore()
    greet = [(doc, place(*peer, 0)) for peer in PEERS] + [(doc, place(0, 0, 1))]
    greet += [(lax.rem(x + dx, 4) * 2 + hi, me) for dx in (1, 2, 3)]
    y_next = (x * 2 + 1 - hi, place(0, 1, 0))
    greet.append(y_next)
    for device in greet:
        pl.semaphore_signal(barrier, inc=1, device_id=device, device_id_type=MESH)

    counter = [0]
    sent = []

    def send(src, dst, device):
        i = counter[0]
        counter[0] += 1
        copy = pltpu.make_async_remote_copy(
            src_ref=src, dst_ref=dst, send_sem=send_sem.at[i], recv_sem=recv_sem.at[i],
            device_id=device, device_id_type=MESH,
        )
        copy.start()
        sent.append(copy)
        return copy

    up, down = (doc, place(1, 0, 0)), (doc, place(3, 0, 0))
    twin_id, y_id = (doc, place(0, 0, 1)), (doc, place(0, 1, 0))
    core_copy, y_copy, z_copy = {}, {}, {}

    def project(j):
        for copy in loads(j):
            copy.wait()

        def one(r):
            docs = (1 - core if r else core) * OWNED
            a = jnp.concatenate([act_v[j, docs + d] for d in range(OWNED)], axis=1)
            g = jnp.concatenate([grad_v[j, docs + d] for d in range(OWNED)], axis=1)
            o_rows, i_rows = dot(pout_v[...], g), dot(pin_v[...], a)
            for d in range(OWNED):
                blocks[j, r, d * SEQ : d * SEQ + RANK] = o_rows[:, d * SEQ : (d + 1) * SEQ]
                blocks[j, r, d * SEQ + RANK : (d + 1) * SEQ] = i_rows[:, d * SEQ : (d + 1) * SEQ]

        one(1)
        core_copy[j] = send(blocks.at[j, 1], twin.at[j], twin_id)
        one(0)

    def ref(t, dz, half):
        if t < 2:
            return blocks.at[PLACE[dz, t], 0, pl.ds(half * HALF_A, HALF_A)]
        return blocks.at[PLACE[dz, 1], 0, pl.ds(PART_A + half * HALF_B, HALF_B)]

    def far(t, half):
        return f_a.at[t, half] if t < 2 else f_b.at[half]

    def near(t, side, half):
        return n_a.at[t, side, half] if t < 2 else n_b.at[side, half]

    def send_far(t):
        z_copy[t, "f0"] = send(ref(t, 2, 0), far(t, 0), up)
        z_copy[t, "f1"] = send(ref(t, 2, 1), far(t, 1), down)

    def send_up_now(t):
        z_copy[t, "u1"] = send(ref(t, 1, 1), near(t, 0, 1), up)

    def send_down_now(t):
        z_copy[t, "d0"] = send(ref(t, 3, 0), near(t, 1, 0), down)

    def send_up_sum(t):
        z_copy[t, "f0"].wait_recv()
        ref(t, 1, 0)[...] += far(t, 0)[...]
        z_copy[t, "u0"] = send(ref(t, 1, 0), near(t, 0, 0), up)

    def send_down_sum(t):
        z_copy[t, "f1"].wait_recv()
        ref(t, 3, 1)[...] += far(t, 1)[...]
        z_copy[t, "d1"] = send(ref(t, 3, 1), near(t, 1, 1), down)

    def finish(t):
        for name in ("u1", "d0", "u0", "d1"):
            z_copy[t, name].wait_recv()
        for half in (0, 1):
            ref(t, 0, half)[...] += near(t, 0, half)[...] + near(t, 1, half)[...]

    def collect(j):
        dz, own = ORDER[j]
        core_copy[j].wait_recv()
        blocks[j, 0] += twin[j]
        if not own:
            y_copy[dz] = send(blocks.at[j, 0, pl.ds(PART_A, ROWS - PART_A)], y_b.at[dz], y_id)
        if dz == 2:
            send_far(own)
        elif dz == 1:
            send_up_now(own)
        elif dz == 3:
            send_down_now(own)

    def y_sum(dz):
        y_copy[dz].wait_recv()
        blocks[PLACE[dz, 1], 0, PART_A:ROWS] += y_b[dz]

    slot = me // 2
    t_copy, t_twin, t_y, t_x = [], [], [], {}

    def piece(k):
        return queries.at[:, pl.ds(pl.multiple_of(WIDE * k, WIDE), WIDE)]

    own_piece = pltpu.make_async_copy(piece(part(0, 0)), t_all.at[core, doc, slot], small_sem.at[len(small)])

    def spread(g, device):
        block = t_all.at[core, g]
        return send(block, block, device)

    def share(g):
        t_twin.append(spread(g, twin_id))

    def x_id(dx):
        return (lax.rem(x + dx, 4) * 2 + hi, me)

    def x_doc(dx, half):
        return 2 * lax.rem(x + 4 - dx, 4) + (1 - hi if half else hi)

    def spread_queries():
        own_piece.start()
        for peer in PEERS:
            t_copy.append(send(piece(part(*peer)), t_all.at[core, doc, slot], (doc, place(*peer, 0))))

    def spread_own():
        own_piece.wait()
        for copy in t_copy:
            copy.wait_recv()
        t_y.append(spread(doc, y_next))
        for dx in (2, 1, 3):
            t_x[dx, 0] = spread(doc, x_id(dx))
        share(doc)

    def spread_other():
        t_y[0].wait_recv()
        for dx in (1, 3):
            t_x[dx, 1] = spread(x_doc(0, 1), x_id(dx))
        share(x_doc(0, 1))

    def spread_far():
        t_x[2, 0].wait_recv()
        t_y.append(spread(x_doc(2, 0), y_next))
        share(x_doc(2, 0))

    def spread_twin(half):
        for dx in (1, 3):
            t_x[dx, half].wait_recv()
            share(x_doc(dx, half))

    def spread_last():
        spread_twin(1)
        t_y[1].wait_recv()
        share(x_doc(2, 1))

    def chunk(j):
        if j + AHEAD < len(ORDER):
            for copy in loads(j + AHEAD):
                copy.start()
        project(j)

    pl.semaphore_wait(barrier, len(greet))
    spread_queries()
    for copy in small[:2]:
        copy.wait()
    chunk(0)
    chunk(1)
    collect(0)
    chunk(2)
    collect(1)
    chunk(3)
    collect(2)
    spread_own()
    chunk(4)
    collect(3)
    send_up_sum(0)
    chunk(5)
    collect(4)
    send_down_sum(0)
    y_sum(2)
    send_far(2)
    chunk(6)
    collect(5)
    send_up_sum(1)
    send_down_sum(1)
    chunk(7)
    collect(6)
    collect(7)
    spread_other()
    y_sum(1)
    send_up_now(2)
    finish(0)
    last = send(blocks.at[PLACE[0, 0], 0, pl.ds(0, PART_A)], y_a, y_id)
    spread_far()
    y_sum(3)
    send_down_now(2)
    spread_twin(0)
    send_up_sum(2)
    send_down_sum(2)
    finish(1)
    for copy in small[2:]:
        copy.wait()
    r_, c_ = iota((RANK, RANK), 0), iota((RANK, RANK), 1)
    odd = (r_ >= 32).astype(jnp.int32)
    pick = jnp.where(c_ == 2 * (r_ - 32 * odd) + odd, 1.0, 0.0)
    none = jnp.zeros((RANK, RANK), F32)
    p_high, p_low = split(
        jnp.concatenate(
            [
                jnp.concatenate([dot(pick, left_v[...], (1, 1), precision=HIGHEST), none], axis=1),
                jnp.concatenate([none, right_v[...]], axis=1),
            ],
            axis=0,
        )
    )
    home = PLACE[0, 1]
    lane = iota((32, 128), 1)

    def gradients(docs):
        cols = jnp.concatenate([blocks[home, 0, d * SEQ : (d + 1) * SEQ] for d in docs], axis=1)
        high, low = split(cols)
        cols = dot(p_high, high) + (dot(p_high, low) + dot(p_low, high))
        for i, d in enumerate(docs):
            row = me * OWNED + d
            weight = jnp.where(iota((1, SEQ), 1) < len_s[row], mask_v[pl.ds(row, 1), :].astype(F32), 0.0)
            o_rows = cols[:RANK, i * SEQ : (i + 1) * SEQ] * weight
            i_rows = cols[RANK:, i * SEQ : (i + 1) * SEQ]
            prod = dot(jnp.concatenate(split(o_rows), axis=0), jnp.concatenate(split(i_rows), axis=0), (1, 1))
            prod = prod[:RANK] + prod[RANK:]
            prod = prod + pltpu.roll(prod, RANK, 1)
            whole = jnp.where(lane < RANK, prod[:32], prod[32:])
            for k in range(8):
                g_own[k, SLICE * d : SLICE * (d + 1)] = whole[SLICE * k : SLICE * (k + 1)]

    last.wait_recv()
    blocks[home, 0, 0:PART_A] += y_a[...]
    gradients((0, 1))
    y_sum(0)
    finish(2)
    gradients((2, 3))

    g_copy = []
    mine = pl.ds(pl.multiple_of(slot * 16, 16), 16)
    for peer in PEERS:
        g_copy.append(send(g_own.at[part(*peer)], g_all.at[mine], (doc, place(*peer, 0))))
    g_all[mine, :] = g_own[part(0, 0)]

    spread_last()
    for copy in t_twin:
        copy.wait_recv()
    rows = jnp.stack([t_all[c].reshape(RANK, 8, WIDE) for c in (0, 1)], axis=1).reshape(1024, WIDE)
    t_high[...], t_low[...] = split(rows)
    early = [copy for copy in sent if not any(copy is other for other in g_copy)]
    for copy in early:
        copy.wait_send()
    for copy in g_copy:
        copy.wait_recv()

    docs = jnp.concatenate([g_all[pl.ds(m, 32, stride=SLICE), :] for m in range(SLICE)], axis=1)
    high, low = split(docs)
    scores = dot(jnp.concatenate([high, low], axis=0), t_high[...], (1, 1))
    scores = scores[:32] + scores[32:] + dot(high, t_low[...], (1, 1))
    for k in range(8):
        s_own[k] = scores[OWNED * k : OWNED * (k + 1)]
    s_copy = []
    for dz, dy in PEERS:
        param = place(dz, dy, 0)
        s_copy.append(send(s_own.at[param // 2], s_all.at[slot], (doc, param)))
    s_all[slot] = s_own[slot]
    for copy in s_copy:
        copy.wait_recv()
    total = s_all[0]
    for k in range(1, 8):
        total = total + s_all[k]
    out[...] = total
    for copy in g_copy + s_copy:
        copy.wait_send()


def body(activations, out_grads, proj_in, proj_out, lengths, loss_mask, queries, left_pre, right_pre):
    wide_in, wide_out = activations.shape[-1], out_grads.shape[-1]
    activations, out_grads = activations.transpose(0, 2, 1), out_grads.transpose(0, 2, 1)
    vmem = pltpu.VMEM
    return pl.pallas_call(
        kernel,
        out_shape=pltpu.VMEM((OWNED, 1024), F32),
        in_specs=[pl.BlockSpec(memory_space=pl.ANY)] * 9,
        out_specs=pl.BlockSpec(memory_space=pltpu.VMEM),
        scratch_shapes=[
            vmem((8, 2 * OWNED, wide_in, SEQ), BF16),
            vmem((8, 2 * OWNED, wide_out, SEQ), BF16),
            vmem(proj_in.shape, BF16),
            vmem(proj_out.shape, BF16),
            pltpu.SMEM(lengths.shape, jnp.int32),
            vmem(loss_mask.shape, jnp.int32),
            vmem(left_pre.shape, F32),
            vmem(right_pre.shape, F32),
            vmem((8, 2, ROWS, 128), F32),
            vmem((8, ROWS, 128), F32),
            vmem((2, 2, HALF_A, 128), F32),
            vmem((2, 2, 2, HALF_A, 128), F32),
            vmem((2, HALF_B, 128), F32),
            vmem((2, 2, HALF_B, 128), F32),
            vmem((PART_A, 128), F32),
            vmem((4, ROWS - PART_A, 128), F32),
            vmem((2, 8, 8, 8, WIDE), F32),
            vmem((1024, WIDE), BF16),
            vmem((1024, WIDE), BF16),
            vmem((8, SLICE * OWNED, 128), F32),
            vmem((128, 128), F32),
            vmem((8, OWNED, 1024), F32),
            vmem((8, OWNED, 1024), F32),
            pltpu.SemaphoreType.DMA((8, 2)),
            pltpu.SemaphoreType.DMA((7,)),
            pltpu.SemaphoreType.DMA((N_SEMS,)),
            pltpu.SemaphoreType.DMA((N_SEMS,)),
        ],
        compiler_params=pltpu.CompilerParams(
            collective_id=0, has_side_effects=True, vmem_limit_bytes=60 * 1024 * 1024
        ),
        cost_estimate=pl.CostEstimate(flops=1_300_000_000, bytes_accessed=20_000_000, transcendentals=0),
    )(activations, out_grads, proj_in, proj_out, lengths, loss_mask, queries, left_pre, right_pre) * (1.0 / (RANK * SEQ**0.5))


def solution(mesh):
    return jax.shard_map(
        body,
        mesh=mesh,
        in_specs=(
            P("doc", None, "param"),
            P("doc", None, "param"),
            P(None, "param"),
            P(None, "param"),
            P("doc"),
            P("doc", None),
            P(("doc", "param"), None),
            P(),
            P(),
        ),
        out_specs=P(("doc", "param"), None),
        check_vma=False,
    )
```

```python
import functools

import jax
import jax.numpy as jnp
from jax import lax
from jax.experimental import pallas as pl
from jax.experimental.pallas import tpu as pltpu
from jax.sharding import PartitionSpec as P

MESH = pl.DeviceIdType.MESH
F32 = jnp.float32
BF16 = jnp.bfloat16
HIGHEST = lax.Precision.HIGHEST

RANK = 64
SEQ = 128
OWNED = 4
ROWS = OWNED * SEQ
HALF_A = 144
HALF_B = 112
PART_A = 2 * HALF_A
AHEAD = 3
ORDER = ((2, 0), (2, 1), (1, 0), (3, 0), (1, 1), (3, 1), (0, 0), (0, 1))
PLACE = {step: j for j, step in enumerate(ORDER)}
PEERS = ((2, 1), (2, 0), (1, 1), (3, 1), (1, 0), (3, 0), (0, 1))
SLICE = 4
WIDE = SLICE * 128
N_SEMS = 8 + 18 + 5 + 7 + 2 + 5 + 8 + 7 + 7


def iota(shape, dim):
    return lax.broadcasted_iota(jnp.int32, shape, dim)


def split(x):
    high = x.astype(BF16)
    return high, (x - high.astype(F32)).astype(BF16)


def dot(a, b, contract=(1, 0), precision=None):
    return lax.dot_general(
        a, b, (((contract[0],), (contract[1],)), ((), ())), precision=precision, preferred_element_type=F32
    )


def kernel(
    act, grad, pin, pout, lengths, mask, queries, left, right,
    out,
    act_v, grad_v, pin_v, pout_v, len_s, mask_v, left_v, right_v,
    blocks, twin, f_a, n_a, f_b, n_b, y_a, y_b,
    t_all, t_high, t_low, g_own, g_all, s_own, s_all,
    load_sem, small_sem, send_sem, recv_sem,
):
    doc, me = lax.axis_index("doc"), lax.axis_index("param")
    x, hi = doc // 2, lax.rem(doc, 2)
    z, lo, core = me // 4, lax.rem(me // 2, 2), lax.rem(me, 2)

    def place(dz, dy, dc):
        py = 1 - lo if dy else lo
        pc = 1 - core if dc else core
        return lax.rem(z + dz, 4) * 4 + py * 2 + pc

    def part(dz, dy):
        py = 1 - lo if dy else lo
        return lax.rem(z + dz, 4) * 2 + py + hi - 2 * py * hi

    def loads(j):
        dz, own = ORDER[j]
        first = place(dz, 1 - own, 0) // 2 * 2 * OWNED
        found = [
            pltpu.make_async_copy(act.at[pl.ds(first, 2 * OWNED)], act_v.at[j], load_sem.at[j, 0]),
            pltpu.make_async_copy(grad.at[pl.ds(first, 2 * OWNED)], grad_v.at[j], load_sem.at[j, 1]),
        ]
        return found

    barrier = pltpu.get_barrier_semaphore()
    greet = [(doc, place(*peer, 0)) for peer in PEERS] + [(doc, place(0, 0, 1))]
    greet += [(lax.rem(x + dx, 4) * 2 + hi, me) for dx in (1, 2, 3)]
    y_next = (x * 2 + 1 - hi, place(0, 1, 0))
    greet.append(y_next)
    for device in greet:
        pl.semaphore_signal(barrier, inc=1, device_id=device, device_id_type=MESH)

    small = [
        pltpu.make_async_copy(src, dst, small_sem.at[i])
        for i, (src, dst) in enumerate(
            (
                (pout, pout_v), (pin, pin_v), (left, left_v), (right, right_v), (mask, mask_v), (lengths, len_s),
            )
        )
    ]
    for copy in loads(0) + small:
        copy.start()
    for j in range(1, AHEAD):
        for copy in loads(j):
            copy.start()

    counter = [0]
    sent = []

    def send(src, dst, device):
        i = counter[0]
        counter[0] += 1
        copy = pltpu.make_async_remote_copy(
            src_ref=src, dst_ref=dst, send_sem=send_sem.at[i], recv_sem=recv_sem.at[i],
            device_id=device, device_id_type=MESH,
        )
        copy.start()
        sent.append(copy)
        return copy

    up, down = (doc, place(1, 0, 0)), (doc, place(3, 0, 0))
    twin_id, y_id = (doc, place(0, 0, 1)), (doc, place(0, 1, 0))
    core_copy, y_copy, z_copy = {}, {}, {}

    def project(j):
        for copy in loads(j):
            copy.wait()

        def one(r):
            docs = (1 - core if r else core) * OWNED
            a = jnp.concatenate([act_v[j, docs + d] for d in range(OWNED)], axis=1)
            g = jnp.concatenate([grad_v[j, docs + d] for d in range(OWNED)], axis=1)
            o_rows, i_rows = dot(pout_v[...], g), dot(pin_v[...], a)
            for d in range(OWNED):
                blocks[j, r, d * SEQ : d * SEQ + RANK] = o_rows[:, d * SEQ : (d + 1) * SEQ]
                blocks[j, r, d * SEQ + RANK : (d + 1) * SEQ] = i_rows[:, d * SEQ : (d + 1) * SEQ]

        one(1)
        core_copy[j] = send(blocks.at[j, 1], twin.at[j], twin_id)
        one(0)

    def ref(t, dz, half):
        if t < 2:
            return blocks.at[PLACE[dz, t], 0, pl.ds(half * HALF_A, HALF_A)]
        return blocks.at[PLACE[dz, 1], 0, pl.ds(PART_A + half * HALF_B, HALF_B)]

    def far(t, half):
        return f_a.at[t, half] if t < 2 else f_b.at[half]

    def near(t, side, half):
        return n_a.at[t, side, half] if t < 2 else n_b.at[side, half]

    def send_far(t):
        z_copy[t, "f0"] = send(ref(t, 2, 0), far(t, 0), up)
        z_copy[t, "f1"] = send(ref(t, 2, 1), far(t, 1), down)

    def send_up_now(t):
        z_copy[t, "u1"] = send(ref(t, 1, 1), near(t, 0, 1), up)

    def send_down_now(t):
        z_copy[t, "d0"] = send(ref(t, 3, 0), near(t, 1, 0), down)

    def send_up_sum(t):
        z_copy[t, "f0"].wait_recv()
        ref(t, 1, 0)[...] += far(t, 0)[...]
        z_copy[t, "u0"] = send(ref(t, 1, 0), near(t, 0, 0), up)

    def send_down_sum(t):
        z_copy[t, "f1"].wait_recv()
        ref(t, 3, 1)[...] += far(t, 1)[...]
        z_copy[t, "d1"] = send(ref(t, 3, 1), near(t, 1, 1), down)

    def finish(t):
        for name in ("u1", "d0", "u0", "d1"):
            z_copy[t, name].wait_recv()
        for half in (0, 1):
            ref(t, 0, half)[...] += near(t, 0, half)[...] + near(t, 1, half)[...]

    def collect(j):
        dz, own = ORDER[j]
        core_copy[j].wait_recv()
        blocks[j, 0] += twin[j]
        if not own:
            y_copy[dz] = send(blocks.at[j, 0, pl.ds(PART_A, ROWS - PART_A)], y_b.at[dz], y_id)
        if dz == 2:
            send_far(own)
        elif dz == 1:
            send_up_now(own)
        elif dz == 3:
            send_down_now(own)

    def y_sum(dz):
        y_copy[dz].wait_recv()
        blocks[PLACE[dz, 1], 0, PART_A:ROWS] += y_b[dz]

    slot = me // 2
    t_copy, t_twin, t_y, t_x = [], [], [], {}

    def piece(k):
        return queries.at[:, pl.ds(pl.multiple_of(WIDE * k, WIDE), WIDE)]

    own_piece = pltpu.make_async_copy(piece(part(0, 0)), t_all.at[core, doc, slot], small_sem.at[len(small)])

    def spread(g, device):
        block = t_all.at[core, g]
        return send(block, block, device)

    def share(g):
        t_twin.append(spread(g, twin_id))

    def x_id(dx):
        return (lax.rem(x + dx, 4) * 2 + hi, me)

    def x_doc(dx, half):
        return 2 * lax.rem(x + 4 - dx, 4) + (1 - hi if half else hi)

    def spread_queries():
        own_piece.start()
        for peer in PEERS:
            t_copy.append(send(piece(part(*peer)), t_all.at[core, doc, slot], (doc, place(*peer, 0))))

    def spread_own():
        own_piece.wait()
        for copy in t_copy:
            copy.wait_recv()
        t_y.append(spread(doc, y_next))
        for dx in (2, 1, 3):
            t_x[dx, 0] = spread(doc, x_id(dx))
        share(doc)

    def spread_other():
        t_y[0].wait_recv()
        for dx in (1, 3):
            t_x[dx, 1] = spread(x_doc(0, 1), x_id(dx))
        share(x_doc(0, 1))

    def spread_far():
        t_x[2, 0].wait_recv()
        t_y.append(spread(x_doc(2, 0), y_next))
        share(x_doc(2, 0))

    def spread_twin(half):
        for dx in (1, 3):
            t_x[dx, half].wait_recv()
            share(x_doc(dx, half))

    def spread_last():
        spread_twin(1)
        t_y[1].wait_recv()
        share(x_doc(2, 1))

    def chunk(j):
        if j + AHEAD < len(ORDER):
            for copy in loads(j + AHEAD):
                copy.start()
        project(j)

    pl.semaphore_wait(barrier, len(greet))
    spread_queries()
    for copy in small[:2]:
        copy.wait()
    chunk(0)
    chunk(1)
    collect(0)
    chunk(2)
    collect(1)
    chunk(3)
    collect(2)
    spread_own()
    chunk(4)
    collect(3)
    send_up_sum(0)
    chunk(5)
    collect(4)
    send_down_sum(0)
    y_sum(2)
    send_far(2)
    chunk(6)
    collect(5)
    send_up_sum(1)
    send_down_sum(1)
    chunk(7)
    collect(6)
    collect(7)
    spread_other()
    y_sum(1)
    send_up_now(2)
    finish(0)
    last = send(blocks.at[PLACE[0, 0], 0, pl.ds(0, PART_A)], y_a, y_id)
    spread_far()
    y_sum(3)
    send_down_now(2)
    spread_twin(0)
    send_up_sum(2)
    send_down_sum(2)
    finish(1)
    for copy in small[2:]:
        copy.wait()
    r_, c_ = iota((RANK, RANK), 0), iota((RANK, RANK), 1)
    odd = (r_ >= 32).astype(jnp.int32)
    pick = jnp.where(c_ == 2 * (r_ - 32 * odd) + odd, 1.0, 0.0)
    none = jnp.zeros((RANK, RANK), F32)
    p_high, p_low = split(
        jnp.concatenate(
            [
                jnp.concatenate([dot(pick, left_v[...], (1, 1), precision=HIGHEST), none], axis=1),
                jnp.concatenate([none, right_v[...]], axis=1),
            ],
            axis=0,
        )
    )
    home = PLACE[0, 1]
    lane = iota((32, 128), 1)

    def gradients(docs):
        cols = jnp.concatenate([blocks[home, 0, d * SEQ : (d + 1) * SEQ] for d in docs], axis=1)
        high, low = split(cols)
        cols = dot(p_high, high) + (dot(p_high, low) + dot(p_low, high))
        for i, d in enumerate(docs):
            row = me * OWNED + d
            weight = jnp.where(iota((1, SEQ), 1) < len_s[row], mask_v[pl.ds(row, 1), :].astype(F32), 0.0)
            o_rows = cols[:RANK, i * SEQ : (i + 1) * SEQ] * weight
            i_rows = cols[RANK:, i * SEQ : (i + 1) * SEQ]
            prod = dot(jnp.concatenate(split(o_rows), axis=0), jnp.concatenate(split(i_rows), axis=0), (1, 1))
            prod = prod[:RANK] + prod[RANK:]
            prod = prod + pltpu.roll(prod, RANK, 1)
            whole = jnp.where(lane < RANK, prod[:32], prod[32:])
            for k in range(8):
                g_own[k, SLICE * d : SLICE * (d + 1)] = whole[SLICE * k : SLICE * (k + 1)]

    last.wait_recv()
    blocks[home, 0, 0:PART_A] += y_a[...]
    gradients((0, 1))
    y_sum(0)
    finish(2)
    gradients((2, 3))

    g_copy = []
    mine = pl.ds(pl.multiple_of(slot * 16, 16), 16)
    for peer in PEERS:
        g_copy.append(send(g_own.at[part(*peer)], g_all.at[mine], (doc, place(*peer, 0))))
    g_all[mine, :] = g_own[part(0, 0)]

    done = len(sent)
    for copy in sent[:done]:
        copy.wait_send()
    spread_last()
    for copy in sent[done:]:
        copy.wait_send()
    for copy in t_twin:
        copy.wait_recv()
    rows = jnp.stack([t_all[c].reshape(RANK, 8, WIDE) for c in (0, 1)], axis=1).reshape(1024, WIDE)
    t_high[...], t_low[...] = split(rows)
    for copy in g_copy:
        copy.wait_recv()

    docs = jnp.concatenate([g_all[pl.ds(m, 32, stride=SLICE), :] for m in range(SLICE)], axis=1)
    high, low = split(docs)
    scores = dot(jnp.concatenate([high, low], axis=0), t_high[...], (1, 1))
    scores = scores[:32] + scores[32:] + dot(high, t_low[...], (1, 1))
    for k in range(8):
        s_own[k] = scores[OWNED * k : OWNED * (k + 1)]
    s_copy = []
    for dz, dy in PEERS:
        param = place(dz, dy, 0)
        s_copy.append(send(s_own.at[param // 2], s_all.at[slot], (doc, param)))
    s_all[slot] = s_own[slot]
    for copy in s_copy:
        copy.wait_send()
    for copy in s_copy:
        copy.wait_recv()
    total = s_all[0]
    for k in range(1, 8):
        total = total + s_all[k]
    out[...] = total


def body(activations, out_grads, proj_in, proj_out, lengths, loss_mask, queries, left_pre, right_pre):
    wide_in, wide_out = activations.shape[-1], out_grads.shape[-1]
    activations, out_grads = activations.transpose(0, 2, 1), out_grads.transpose(0, 2, 1)
    vmem = pltpu.VMEM
    return pl.pallas_call(
        kernel,
        out_shape=pltpu.VMEM((OWNED, 1024), F32),
        in_specs=[pl.BlockSpec(memory_space=pl.ANY)] * 9,
        out_specs=pl.BlockSpec(memory_space=pltpu.VMEM),
        scratch_shapes=[
            vmem((8, 2 * OWNED, wide_in, SEQ), BF16),
            vmem((8, 2 * OWNED, wide_out, SEQ), BF16),
            vmem(proj_in.shape, BF16),
            vmem(proj_out.shape, BF16),
            pltpu.SMEM(lengths.shape, jnp.int32),
            vmem(loss_mask.shape, jnp.int32),
            vmem(left_pre.shape, F32),
            vmem(right_pre.shape, F32),
            vmem((8, 2, ROWS, 128), F32),
            vmem((8, ROWS, 128), F32),
            vmem((2, 2, HALF_A, 128), F32),
            vmem((2, 2, 2, HALF_A, 128), F32),
            vmem((2, HALF_B, 128), F32),
            vmem((2, 2, HALF_B, 128), F32),
            vmem((PART_A, 128), F32),
            vmem((4, ROWS - PART_A, 128), F32),
            vmem((2, 8, 8, 8, WIDE), F32),
            vmem((1024, WIDE), BF16),
            vmem((1024, WIDE), BF16),
            vmem((8, SLICE * OWNED, 128), F32),
            vmem((136, 128), F32),
            vmem((8, OWNED, 1024), F32),
            vmem((8, OWNED, 1024), F32),
            pltpu.SemaphoreType.DMA((8, 2)),
            pltpu.SemaphoreType.DMA((7,)),
            pltpu.SemaphoreType.DMA((N_SEMS,)),
            pltpu.SemaphoreType.DMA((N_SEMS,)),
        ],
        compiler_params=pltpu.CompilerParams(
            collective_id=0, has_side_effects=True, vmem_limit_bytes=60 * 1024 * 1024
        ),
        cost_estimate=pl.CostEstimate(flops=1_300_000_000, bytes_accessed=20_000_000, transcendentals=0),
    )(activations, out_grads, proj_in, proj_out, lengths, loss_mask, queries, left_pre, right_pre) * (1.0 / (RANK * SEQ**0.5))


def solution(mesh):
    return jax.shard_map(
        body,
        mesh=mesh,
        in_specs=(
            P("doc", None, "param"),
            P("doc", None, "param"),
            P(None, "param"),
            P(None, "param"),
            P("doc"),
            P("doc", None),
            P(("doc", "param"), None),
            P(),
            P(),
        ),
        out_specs=P(("doc", "param"), None),
        check_vma=False,
    )
```

```python
import functools

import jax
import jax.numpy as jnp
from jax import lax
from jax.experimental import pallas as pl
from jax.experimental.pallas import tpu as pltpu
from jax.sharding import PartitionSpec as P

MESH = pl.DeviceIdType.MESH
F32 = jnp.float32
BF16 = jnp.bfloat16
HIGHEST = lax.Precision.HIGHEST

RANK = 64
SEQ = 128
OWNED = 4
ROWS = OWNED * SEQ
HALF_A = 144
HALF_B = 112
PART_A = 2 * HALF_A
AHEAD = 3
ORDER = ((2, 0), (2, 1), (1, 0), (3, 0), (1, 1), (3, 1), (0, 0), (0, 1))
PLACE = {step: j for j, step in enumerate(ORDER)}
PEERS = ((2, 1), (2, 0), (1, 1), (3, 1), (1, 0), (3, 0), (0, 1))
SLICE = 4
WIDE = SLICE * 128
N_SEMS = 8 + 18 + 5 + 7 + 2 + 5 + 8 + 7 + 7


def iota(shape, dim):
    return lax.broadcasted_iota(jnp.int32, shape, dim)


def split(x):
    high = x.astype(BF16)
    return high, (x - high.astype(F32)).astype(BF16)


def dot(a, b, contract=(1, 0), precision=None):
    return lax.dot_general(
        a, b, (((contract[0],), (contract[1],)), ((), ())), precision=precision, preferred_element_type=F32
    )


def kernel(
    act, grad, pin, pout, lengths, mask, queries, left, right,
    out,
    act_v, grad_v, pin_v, pout_v, len_s, mask_v, left_v, right_v,
    blocks, twin, f_a, n_a, f_b, n_b, y_a, y_b,
    t_all, t_high, t_low, g_own, g_all, s_own, s_all,
    load_sem, small_sem, send_sem, recv_sem,
):
    doc, me = lax.axis_index("doc"), lax.axis_index("param")
    x, hi = doc // 2, lax.rem(doc, 2)
    z, lo, core = me // 4, lax.rem(me // 2, 2), lax.rem(me, 2)

    def place(dz, dy, dc):
        py = 1 - lo if dy else lo
        pc = 1 - core if dc else core
        return lax.rem(z + dz, 4) * 4 + py * 2 + pc

    def part(dz, dy):
        py = 1 - lo if dy else lo
        return lax.rem(z + dz, 4) * 2 + py + hi - 2 * py * hi

    def loads(j):
        dz, own = ORDER[j]
        first = place(dz, 1 - own, 0) // 2 * 2 * OWNED
        found = [
            pltpu.make_async_copy(act.at[pl.ds(first, 2 * OWNED)], act_v.at[j], load_sem.at[j, 0]),
            pltpu.make_async_copy(grad.at[pl.ds(first, 2 * OWNED)], grad_v.at[j], load_sem.at[j, 1]),
        ]
        return found

    barrier = pltpu.get_barrier_semaphore()
    greet = [(doc, place(*peer, 0)) for peer in PEERS] + [(doc, place(0, 0, 1))]
    greet += [(lax.rem(x + dx, 4) * 2 + hi, me) for dx in (1, 2, 3)]
    y_next = (x * 2 + 1 - hi, place(0, 1, 0))
    greet.append(y_next)
    for device in greet:
        pl.semaphore_signal(barrier, inc=1, device_id=device, device_id_type=MESH)

    small = [
        pltpu.make_async_copy(src, dst, small_sem.at[i])
        for i, (src, dst) in enumerate(
            (
                (pout, pout_v), (pin, pin_v), (left, left_v), (right, right_v), (mask, mask_v), (lengths, len_s),
            )
        )
    ]
    for copy in loads(0) + small:
        copy.start()
    for j in range(1, AHEAD):
        for copy in loads(j):
            copy.start()

    counter = [0]
    sent = []

    def send(src, dst, device):
        i = counter[0]
        counter[0] += 1
        copy = pltpu.make_async_remote_copy(
            src_ref=src, dst_ref=dst, send_sem=send_sem.at[i], recv_sem=recv_sem.at[i],
            device_id=device, device_id_type=MESH,
        )
        copy.start()
        sent.append(copy)
        return copy

    up, down = (doc, place(1, 0, 0)), (doc, place(3, 0, 0))
    twin_id, y_id = (doc, place(0, 0, 1)), (doc, place(0, 1, 0))
    core_copy, y_copy, z_copy = {}, {}, {}

    def project(j):
        for copy in loads(j):
            copy.wait()

        def one(r):
            docs = (1 - core if r else core) * OWNED
            a = jnp.concatenate([act_v[j, docs + d] for d in range(OWNED)], axis=1)
            g = jnp.concatenate([grad_v[j, docs + d] for d in range(OWNED)], axis=1)
            o_rows, i_rows = dot(pout_v[...], g), dot(pin_v[...], a)
            for d in range(OWNED):
                blocks[j, r, d * SEQ : d * SEQ + RANK] = o_rows[:, d * SEQ : (d + 1) * SEQ]
                blocks[j, r, d * SEQ + RANK : (d + 1) * SEQ] = i_rows[:, d * SEQ : (d + 1) * SEQ]

        one(1)
        core_copy[j] = send(blocks.at[j, 1], twin.at[j], twin_id)
        one(0)

    def ref(t, dz, half):
        if t < 2:
            return blocks.at[PLACE[dz, t], 0, pl.ds(half * HALF_A, HALF_A)]
        return blocks.at[PLACE[dz, 1], 0, pl.ds(PART_A + half * HALF_B, HALF_B)]

    def far(t, half):
        return f_a.at[t, half] if t < 2 else f_b.at[half]

    def near(t, side, half):
        return n_a.at[t, side, half] if t < 2 else n_b.at[side, half]

    def send_far(t):
        z_copy[t, "f0"] = send(ref(t, 2, 0), far(t, 0), up)
        z_copy[t, "f1"] = send(ref(t, 2, 1), far(t, 1), down)

    def send_up_now(t):
        z_copy[t, "u1"] = send(ref(t, 1, 1), near(t, 0, 1), up)

    def send_down_now(t):
        z_copy[t, "d0"] = send(ref(t, 3, 0), near(t, 1, 0), down)

    def send_up_sum(t):
        z_copy[t, "f0"].wait_recv()
        ref(t, 1, 0)[...] += far(t, 0)[...]
        z_copy[t, "u0"] = send(ref(t, 1, 0), near(t, 0, 0), up)

    def send_down_sum(t):
        z_copy[t, "f1"].wait_recv()
        ref(t, 3, 1)[...] += far(t, 1)[...]
        z_copy[t, "d1"] = send(ref(t, 3, 1), near(t, 1, 1), down)

    def finish(t):
        for name in ("u1", "d0", "u0", "d1"):
            z_copy[t, name].wait_recv()
        for half in (0, 1):
            ref(t, 0, half)[...] += near(t, 0, half)[...] + near(t, 1, half)[...]

    def collect(j):
        dz, own = ORDER[j]
        core_copy[j].wait_recv()
        blocks[j, 0] += twin[j]
        if not own:
            y_copy[dz] = send(blocks.at[j, 0, pl.ds(PART_A, ROWS - PART_A)], y_b.at[dz], y_id)
        if dz == 2:
            send_far(own)
        elif dz == 1:
            send_up_now(own)
        elif dz == 3:
            send_down_now(own)

    def y_sum(dz):
        y_copy[dz].wait_recv()
        blocks[PLACE[dz, 1], 0, PART_A:ROWS] += y_b[dz]

    slot = me // 2
    t_copy, t_twin, t_y, t_x = [], [], [], {}

    def piece(k):
        return queries.at[:, pl.ds(pl.multiple_of(WIDE * k, WIDE), WIDE)]

    own_piece = pltpu.make_async_copy(piece(part(0, 0)), t_all.at[core, doc, slot], small_sem.at[len(small)])

    def spread(g, device):
        block = t_all.at[core, g]
        return send(block, block, device)

    def share(g):
        t_twin.append(spread(g, twin_id))

    def x_id(dx):
        return (lax.rem(x + dx, 4) * 2 + hi, me)

    def x_doc(dx, half):
        return 2 * lax.rem(x + 4 - dx, 4) + (1 - hi if half else hi)

    def spread_queries():
        own_piece.start()
        for peer in PEERS:
            t_copy.append(send(piece(part(*peer)), t_all.at[core, doc, slot], (doc, place(*peer, 0))))

    def spread_own():
        own_piece.wait()
        for copy in t_copy:
            copy.wait_recv()
        t_y.append(spread(doc, y_next))
        for dx in (2, 1, 3):
            t_x[dx, 0] = spread(doc, x_id(dx))
        share(doc)

    def spread_other():
        t_y[0].wait_recv()
        for dx in (1, 3):
            t_x[dx, 1] = spread(x_doc(0, 1), x_id(dx))
        share(x_doc(0, 1))

    def spread_far():
        t_x[2, 0].wait_recv()
        t_y.append(spread(x_doc(2, 0), y_next))
        share(x_doc(2, 0))

    def spread_twin(half):
        for dx in (1, 3):
            t_x[dx, half].wait_recv()
            share(x_doc(dx, half))

    def spread_last():
        spread_twin(1)
        t_y[1].wait_recv()
        share(x_doc(2, 1))

    def chunk(j):
        if j + AHEAD < len(ORDER):
            for copy in loads(j + AHEAD):
                copy.start()
        project(j)

    pl.semaphore_wait(barrier, len(greet))
    spread_queries()
    for copy in small[:2]:
        copy.wait()
    chunk(0)
    chunk(1)
    collect(0)
    chunk(2)
    collect(1)
    chunk(3)
    collect(2)
    spread_own()
    chunk(4)
    collect(3)
    y_sum(2)
    send_far(2)
    send_up_sum(0)
    send_down_sum(0)
    chunk(5)
    collect(4)
    chunk(6)
    collect(5)
    send_up_sum(1)
    send_down_sum(1)
    chunk(7)
    collect(6)
    collect(7)
    spread_other()
    y_sum(1)
    send_up_now(2)
    finish(0)
    last = send(blocks.at[PLACE[0, 0], 0, pl.ds(0, PART_A)], y_a, y_id)
    y_sum(3)
    send_down_now(2)
    send_up_sum(2)
    send_down_sum(2)
    spread_far()
    spread_twin(0)
    finish(1)
    for copy in small[2:]:
        copy.wait()
    r_, c_ = iota((RANK, RANK), 0), iota((RANK, RANK), 1)
    odd = (r_ >= 32).astype(jnp.int32)
    pick = jnp.where(c_ == 2 * (r_ - 32 * odd) + odd, 1.0, 0.0)
    none = jnp.zeros((RANK, RANK), F32)
    p_high, p_low = split(
        jnp.concatenate(
            [
                jnp.concatenate([dot(pick, left_v[...], (1, 1), precision=HIGHEST), none], axis=1),
                jnp.concatenate([none, right_v[...]], axis=1),
            ],
            axis=0,
        )
    )
    home = PLACE[0, 1]
    lane = iota((32, 128), 1)

    def gradients(docs):
        cols = jnp.concatenate([blocks[home, 0, d * SEQ : (d + 1) * SEQ] for d in docs], axis=1)
        high, low = split(cols)
        cols = dot(p_high, high) + (dot(p_high, low) + dot(p_low, high))
        for i, d in enumerate(docs):
            row = me * OWNED + d
            weight = jnp.where(iota((1, SEQ), 1) < len_s[row], mask_v[pl.ds(row, 1), :].astype(F32), 0.0)
            o_rows = cols[:RANK, i * SEQ : (i + 1) * SEQ] * weight
            i_rows = cols[RANK:, i * SEQ : (i + 1) * SEQ]
            prod = dot(jnp.concatenate(split(o_rows), axis=0), jnp.concatenate(split(i_rows), axis=0), (1, 1))
            prod = prod[:RANK] + prod[RANK:]
            prod = prod + pltpu.roll(prod, RANK, 1)
            whole = jnp.where(lane < RANK, prod[:32], prod[32:])
            for k in range(8):
                g_own[k, SLICE * d : SLICE * (d + 1)] = whole[SLICE * k : SLICE * (k + 1)]

    last.wait_recv()
    blocks[home, 0, 0:PART_A] += y_a[...]
    gradients((0, 1))
    y_sum(0)
    finish(2)
    gradients((2, 3))

    g_copy = []
    mine = pl.ds(pl.multiple_of(slot * 16, 16), 16)
    for peer in PEERS:
        g_copy.append(send(g_own.at[part(*peer)], g_all.at[mine], (doc, place(*peer, 0))))
    g_all[mine, :] = g_own[part(0, 0)]

    done = len(sent)
    for copy in sent[:done]:
        copy.wait_send()
    spread_last()
    for copy in sent[done:]:
        copy.wait_send()
    for copy in t_twin:
        copy.wait_recv()
    rows = jnp.stack([t_all[c].reshape(RANK, 8, WIDE) for c in (0, 1)], axis=1).reshape(1024, WIDE)
    t_high[...], t_low[...] = split(rows)
    for copy in g_copy:
        copy.wait_recv()

    docs = jnp.concatenate([g_all[pl.ds(m, 32, stride=SLICE), :] for m in range(SLICE)], axis=1)
    high, low = split(docs)
    scores = dot(jnp.concatenate([high, low], axis=0), t_high[...], (1, 1))
    scores = scores[:32] + scores[32:] + dot(high, t_low[...], (1, 1))
    for k in range(8):
        s_own[k] = scores[OWNED * k : OWNED * (k + 1)]
    s_copy = []
    for dz, dy in PEERS:
        param = place(dz, dy, 0)
        s_copy.append(send(s_own.at[param // 2], s_all.at[slot], (doc, param)))
    s_all[slot] = s_own[slot]
    for copy in s_copy:
        copy.wait_send()
    for copy in s_copy:
        copy.wait_recv()
    total = s_all[0]
    for k in range(1, 8):
        total = total + s_all[k]
    out[...] = total


def body(activations, out_grads, proj_in, proj_out, lengths, loss_mask, queries, left_pre, right_pre):
    wide_in, wide_out = activations.shape[-1], out_grads.shape[-1]
    activations, out_grads = activations.transpose(0, 2, 1), out_grads.transpose(0, 2, 1)
    vmem = pltpu.VMEM
    return pl.pallas_call(
        kernel,
        out_shape=pltpu.VMEM((OWNED, 1024), F32),
        in_specs=[pl.BlockSpec(memory_space=pl.ANY)] * 9,
        out_specs=pl.BlockSpec(memory_space=pltpu.VMEM),
        scratch_shapes=[
            vmem((8, 2 * OWNED, wide_in, SEQ), BF16),
            vmem((8, 2 * OWNED, wide_out, SEQ), BF16),
            vmem(proj_in.shape, BF16),
            vmem(proj_out.shape, BF16),
            pltpu.SMEM(lengths.shape, jnp.int32),
            vmem(loss_mask.shape, jnp.int32),
            vmem(left_pre.shape, F32),
            vmem(right_pre.shape, F32),
            vmem((8, 2, ROWS, 128), F32),
            vmem((8, ROWS, 128), F32),
            vmem((2, 2, HALF_A, 128), F32),
            vmem((2, 2, 2, HALF_A, 128), F32),
            vmem((2, HALF_B, 128), F32),
            vmem((2, 2, HALF_B, 128), F32),
            vmem((PART_A, 128), F32),
            vmem((4, ROWS - PART_A, 128), F32),
            vmem((2, 8, 8, 8, WIDE), F32),
            vmem((1024, WIDE), BF16),
            vmem((1024, WIDE), BF16),
            vmem((8, SLICE * OWNED, 128), F32),
            vmem((136, 128), F32),
            vmem((8, OWNED, 1024), F32),
            vmem((8, OWNED, 1024), F32),
            pltpu.SemaphoreType.DMA((8, 2)),
            pltpu.SemaphoreType.DMA((7,)),
            pltpu.SemaphoreType.DMA((N_SEMS,)),
            pltpu.SemaphoreType.DMA((N_SEMS,)),
        ],
        compiler_params=pltpu.CompilerParams(
            collective_id=0, has_side_effects=True, vmem_limit_bytes=60 * 1024 * 1024
        ),
        cost_estimate=pl.CostEstimate(flops=1_300_000_000, bytes_accessed=20_000_000, transcendentals=0),
    )(activations, out_grads, proj_in, proj_out, lengths, loss_mask, queries, left_pre, right_pre) * (1.0 / (RANK * SEQ**0.5))


def solution(mesh):
    return jax.shard_map(
        body,
        mesh=mesh,
        in_specs=(
            P("doc", None, "param"),
            P("doc", None, "param"),
            P(None, "param"),
            P(None, "param"),
            P("doc"),
            P("doc", None),
            P(("doc", "param"), None),
            P(),
            P(),
        ),
        out_specs=P(("doc", "param"), None),
        check_vma=False,
    )
```
